512 devices in a mesh: seq: 128 (over z, y, core), head: 4 (over x).
Axes of the slice: x: 4, y: 8, z: 8, core: 2. Of those that a mesh axis runs over, the one named last changes fastest.
Arguments:
- queries: bfloat16 [65536, 4096], P('seq', 'head'), may hold values from -6 to 6
- keys: bfloat16 [65536, 4096], P('seq', 'head'), may hold values from -6 to 6
- values: bfloat16 [65536, 4096], P('seq', 'head'), may hold values from -6 to 6
- level_weights: float32 [9, 32, 65536], P(None, 'head', 'seq'), may hold values from 0.1 to 3, as said below
- norm_gain: float32 [4096], P('head'), may hold values from 0.25 to 1.75
Outputs:
- mixed: bfloat16 [65536, 4096], P('seq', 'head')
The draws below stay inside these ranges and needn't reach their ends.
Inputs may be any that keep to these rules, and one draw needn't show every extreme that they name: `level_weights`: positive level weights.
All inputs are finite; a program needn't handle non-finite values.
Results may differ from the reference program's by a relative error of at most 0.0049.
Values may be sent and summed in bfloat16 or wider, within the bound.
A program may use at most 64 MiB of HBM per device.

```python
import math
import jax
import jax.numpy as jnp
from jax import lax

HEADS = 32
HEAD_DIM = 128
STRETCH = 256
D = 4096
TOKENS = 65536
LOCAL_BITS = 1
SEQ_BITS = 7
LEVELS = 9


def draw_level_weights(key, part):
    head_place = jnp.arange(HEADS, dtype=jnp.float32)[None, :, None]
    head_ramp = head_place / (HEADS - 1)
    base_draw = jnp.exp(jax.random.uniform(key, (LEVELS, HEADS, TOKENS), jnp.float32, math.log(0.1), 0.0))
    factor = 1.0 + 2.0 * head_ramp
    return base_draw * factor


def shard_levels(rng, dims, cuts, least, largest):
    factor_of, own = 1.0, jax.random.fold_in(rng, 6)
    for position, parts in cuts:
        heights = jnp.exp(jax.random.uniform(jax.random.fold_in(own, position), (parts,), jnp.float32, least / len(cuts), largest / len(cuts)))
        factor_of = factor_of * jnp.repeat(heights, dims[position] // parts).reshape([-1 if axis == position else 1 for axis in range(len(dims))])
    return factor_of


def gaussian(rng, dims, spread, limit, cuts=(), kind=jnp.bfloat16):
    result = spread * jax.random.normal(rng, dims, jnp.float32)
    if cuts:
        result = result * shard_levels(rng, dims, cuts, -0.22, 0.18)
    return jnp.clip(result, -limit, limit).astype(kind)


def setup_inputs(seed: int = 0) -> dict:
    seeds = jax.random.split(jax.random.key(seed), 6)
    return {
        "queries": gaussian(seeds[0], (TOKENS, D), 1.0, 6.0, ((0, 128), (1, 4))),
        "keys": gaussian(seeds[1], (TOKENS, D), 1.0, 6.0, ((0, 128), (1, 4))),
        "values": gaussian(seeds[2], (TOKENS, D), 1.0, 6.0, ((0, 128), (1, 4))),
        "level_weights": draw_level_weights(jax.random.fold_in(seeds[5], 71), 0),
        "norm_gain": jnp.clip(1.0 + 0.15 * jax.random.normal(seeds[4], (D,), jnp.float32), 0.25, 1.75),
    }


EPSILON = 1e-06
PRECISION_TOP = lax.Precision.HIGHEST

def one_head(pieces):
    query_h, key_h, value_h, weight_h = pieces
    groups_total = TOKENS // STRETCH
    query_block_list = query_h.astype(jnp.float32).reshape(groups_total, STRETCH, HEAD_DIM)
    key_blocks = key_h.astype(jnp.float32).reshape(groups_total, STRETCH, HEAD_DIM)
    value_blocks = value_h.astype(jnp.float32).reshape(groups_total, STRETCH, HEAD_DIM)
    states = jnp.einsum('ctk,ctv->ckv', key_blocks, value_blocks, precision=PRECISION_TOP)
    scores = jnp.einsum('ctk,csk->cts', query_block_list, key_blocks, precision=PRECISION_TOP)
    causal = lax.broadcasted_iota(jnp.int32, (STRETCH, STRETCH), 0) >= lax.broadcasted_iota(jnp.int32, (STRETCH, STRETCH), 1)
    attn_probs = jnp.where(causal[None], scores, jnp.zeros_like(scores)).astype(jnp.bfloat16)
    attn_probs = lax.optimization_barrier(attn_probs).astype(jnp.float32)
    intra_out = jnp.einsum('cts,csv->ctv', attn_probs, value_blocks, precision=PRECISION_TOP)
    combined = weight_h[0].reshape(groups_total, STRETCH)[:, :, None] * intra_out
    running = states
    for level_bit in range(LOCAL_BITS + SEQ_BITS):
        groups = running.shape[0] // 2
        block_span = 2 ** level_bit
        halves = running.reshape(groups, 2, HEAD_DIM, HEAD_DIM)
        leftward_sum = lax.optimization_barrier(halves[:, 0].astype(jnp.bfloat16)).astype(jnp.float32)
        rightward_queries = query_block_list.reshape(groups, 2, block_span * STRETCH, HEAD_DIM)[:, 1]
        state_readout = jnp.einsum('yag,ygq->yaq', rightward_queries, leftward_sum, precision=PRECISION_TOP)
        level_weight = weight_h[1 + level_bit].reshape(groups, 2, block_span * STRETCH)[:, 1]
        contrib = level_weight[:, :, None] * state_readout
        padded = jnp.stack([jnp.zeros_like(contrib), contrib], axis=1)
        combined = combined + padded.reshape(groups_total, STRETCH, HEAD_DIM)
        running = halves[:, 0] + halves[:, 1]
    return combined.reshape(TOKENS, HEAD_DIM)

def reference(queries, keys, values, level_weights, norm_gain):
    query_heads = queries.reshape(TOKENS, HEADS, HEAD_DIM).transpose(1, 0, 2)
    key_heads = keys.reshape(TOKENS, HEADS, HEAD_DIM).transpose(1, 0, 2)
    value_heads = values.reshape(TOKENS, HEADS, HEAD_DIM).transpose(1, 0, 2)
    weight_heads = level_weights.transpose(1, 0, 2)
    per_head = lax.map(one_head, (query_heads, key_heads, value_heads, weight_heads))
    attended = per_head.transpose(1, 0, 2).reshape(TOKENS, D)
    mean_square = lax.optimization_barrier(jnp.mean(attended * attended, axis=1, keepdims=True))
    mixed = attended * lax.rsqrt(mean_square + EPSILON) * norm_gain.astype(jnp.float32)[None, :]
    return mixed.astype(jnp.bfloat16)
```

```python
import jax
import jax.numpy as jnp
from jax import lax
from jax.experimental import pallas as pl
from jax.experimental.pallas import tpu as pltpu
from jax.sharding import PartitionSpec as P

HEAD_DIM = 128
STRETCH = 256
D = 4096
EPSILON = 1e-06

RING = 8
COLS = 4
HEADS_HERE = 8
TOK = 512
HALF = 64
FAR_FIRST = (4, 3, 5, 2, 6, 1, 7)
NEAR_FIRST = (1, 7, 2, 6, 3, 5, 4)
MESH = pl.DeviceIdType.MESH
F32 = jnp.float32
BF16 = jnp.bfloat16


def nt(a, b):
    return lax.dot_general(a, b, (((1,), (1,)), ((), ())), preferred_element_type=F32)


def tn(a, b):
    return lax.dot_general(a, b, (((0,), (0,)), ((), ())), preferred_element_type=F32)


def nn(a, b):
    return jnp.dot(a, b, preferred_element_type=F32)


def kernel(
    q_hbm, k_hbm, v_hbm, w_hbm, g_hbm, out_hbm,
    q_s, k_s, v_s, w_v, g_v, w_rows, w_cols, out_s,
    first, own_sum, own_bf, pair_in, core0, chip_sum, ring_in, ring_sum, totals, low, high,
    acc, sq, sq_in,
    load_sem, misc_sem, out_sem,
    pair_send, pair_recv, core_send, core_recv, ring_send, ring_recv, next_send, next_recv,
    low_send, low_recv, tot_send, tot_recv, high_send, high_recv,
    fwl_send, fwl_recv, fwh_send, fwh_recv, sq_send, sq_recv,
):
    seq = lax.axis_index("seq")
    col = lax.axis_index("head")
    core = lax.rem(seq, 2)
    y = lax.rem(seq // 2, RING)
    z = seq // (2 * RING)

    def device(z_, y_, core_):
        return (z_ * (2 * RING) + y_ * 2 + core_, col)

    sibling = device(z, y, 1 - core)
    mine = pl.ds(pl.multiple_of(core * HALF, HALF), HALF)
    other = pl.ds(pl.multiple_of((1 - core) * HALF, HALF), HALF)

    def row_peer(d):
        return lax.rem(y + d, RING)

    def col_peer(d):
        return lax.rem(z + d, RING)

    def remote(src, dst, send, recv, target):
        return pltpu.make_async_remote_copy(
            src_ref=src, dst_ref=dst, send_sem=send, recv_sem=recv, device_id=target, device_id_type=MESH
        )

    loads = {}
    for name, src, dst, slot in (("k", k_hbm, k_s, 0), ("v", v_hbm, v_s, 1), ("q", q_hbm, q_s, 2)):
        for h in range(HEADS_HERE):
            loads[name, h] = pltpu.make_async_copy(
                src.at[:, pl.ds(h * HEAD_DIM, HEAD_DIM)], dst.at[h], load_sem.at[slot, h]
            )
    for h in range(HEADS_HERE):
        loads["k", h].start()
        loads["v", h].start()
    w_load = pltpu.make_async_copy(w_hbm, w_v, misc_sem.at[0])
    g_load = pltpu.make_async_copy(g_hbm, g_v, misc_sem.at[1])

    barrier = pltpu.get_barrier_semaphore()
    pl.semaphore_signal(barrier, inc=1, device_id=sibling, device_id_type=MESH)
    for d in range(1, RING):
        pl.semaphore_signal(barrier, inc=1, device_id=device(z, row_peer(d), core), device_id_type=MESH)
        pl.semaphore_signal(barrier, inc=1, device_id=device(col_peer(d), y, core), device_id_type=MESH)
    for d in range(1, COLS):
        pl.semaphore_signal(barrier, inc=1, device_id=(seq, lax.rem(col + d, COLS)), device_id_type=MESH)

    for h in range(HEADS_HERE):
        loads["q", h].start()
    w_load.start()
    g_load.start()
    for h in range(HEADS_HERE):
        loads["k", h].wait()
        loads["v", h].wait()

    order = FAR_FIRST + (0,)

    def to_sibling(i, h):
        return remote(own_sum.at[h, other, :], pair_in.at[h], pair_send.at[i], pair_recv.at[i], sibling)

    for i, d in enumerate(order):
        h = row_peer(d)
        k = k_s[h]
        v = v_s[h]
        s0 = tn(k[:STRETCH], v[:STRETCH])
        s1 = tn(k[STRETCH:], v[STRETCH:])
        first[h] = s0.astype(BF16)
        s = s0 + s1
        own_sum[h] = s
        own_bf[h] = s.astype(BF16)
        if i == 0:
            pl.semaphore_wait(barrier, 1 + 2 * (RING - 1) + COLS - 1)
        to_sibling(i, h).start()

    to_core1 = remote(own_bf, core0, core_send, core_recv, sibling)

    @pl.when(core == 0)
    def _():
        to_core1.start()

    def to_owner(d):
        h = row_peer(d)
        return remote(chip_sum.at[h], ring_in.at[y], ring_send.at[d - 1], ring_recv.at[d - 1], device(z, h, core))

    for i, d in enumerate(order):
        h = row_peer(d)
        to_sibling(i, h).wait_recv()
        c = (own_sum[h, mine, :] + pair_in[h]).astype(BF16)
        chip_sum[h] = c
        if d:
            to_owner(d).start()
        else:
            ring_in[y] = c

    to_next = remote(
        chip_sum, low.at[0, :, mine, :], next_send, next_recv, device(z, lax.rem(y + 1, RING), core)
    )
    y0 = lax.rem(y, 2) == 1
    y1 = lax.rem(y // 2, 2) == 1
    y2 = y // 4 == 1

    @pl.when(jnp.logical_not(y0))
    def _():
        to_next.start()

    w_load.wait()
    for h in range(HEADS_HERE):
        for level in range(9):
            w_rows[h, level : level + 1, :] = w_v[level, h : h + 1, :]
        w_rows[h, 9:16, :] = jnp.zeros((7, TOK), F32)
    for h in range(HEADS_HERE):
        w_cols[h] = w_rows[h].T

    for h in range(HEADS_HERE):
        loads["q", h].wait()

    causal = lax.broadcasted_iota(jnp.int32, (STRETCH, STRETCH), 0) >= lax.broadcasted_iota(
        jnp.int32, (STRETCH, STRETCH), 1
    )

    def within(h):
        for s in range(2):
            rows = slice(s * STRETCH, (s + 1) * STRETCH)
            qs = q_s[h, rows, :]
            probs = jnp.where(causal, nt(qs, k_s[h, rows, :]), 0.0).astype(BF16)
            part = w_cols[h, rows, 0:1] * nn(probs, v_s[h, rows, :])
            if s == 1:
                part += w_cols[h, rows, 1:2] * nn(qs, first[h])
            acc[h, rows, :] = part

    for h in range(0, 5):
        within(h)

    for d in range(1, RING):
        to_owner(d).wait_recv()
    part = [ring_in[j].astype(F32) for j in range(RING)]
    s01 = part[0] + part[1]
    s0123 = s01 + (part[2] + part[3])
    s45 = part[4] + part[5]
    total = s0123 + (s45 + (part[6] + part[7]))
    totals[z] = total.astype(BF16)

    def to_column(d):
        return remote(
            totals.at[z], totals.at[z], tot_send.at[d - 1], tot_recv.at[d - 1], device(col_peer(d), y, core)
        )

    for d in FAR_FIRST:
        to_column(d).start()

    ring_sum[0] = s01.astype(BF16)
    ring_sum[1] = s45.astype(BF16)
    ring_sum[2] = s0123.astype(BF16)

    def low_copy(level, d):
        target = row_peer(d)
        src = ring_sum.at[target // 4] if level == 1 else ring_sum.at[2]
        return remote(
            src, low.at[level, y, mine, :], low_send.at[level - 1, d - 1], low_recv.at[level - 1, d - 1],
            device(z, target, core),
        )

    for d in FAR_FIRST:
        target = row_peer(d)

        @pl.when(lax.rem(target // 2, 2) == 1)
        def _():
            low_copy(1, d).start()

        @pl.when(target // 4 == 1)
        def _():
            low_copy(2, d).start()

    @pl.when(y1)
    def _():
        low[1, y, mine, :] = ring_sum[y // 4]

    @pl.when(y2)
    def _():
        low[2, y, mine, :] = ring_sum[2]

    for h in range(5, HEADS_HERE):
        within(h)

    for d in range(1, RING):
        to_column(d).wait_recv()
    zero = jnp.zeros((HALF, HEAD_DIM), F32)
    tot = lambda i: totals[i].astype(F32)
    z_even = z // 2 * 2
    z_four = z // 4 * 4
    odd = lax.rem(z, 2) == 1
    high[y, mine, 0:128] = jnp.where(odd, tot(z_even), zero).astype(BF16)
    high[y, mine, 128:256] = jnp.where(
        lax.rem(z // 2, 2) == 1, tot(z_four) + tot(z_four + 1), zero
    ).astype(BF16)
    high[y, mine, 256:384] = jnp.where(
        z // 4 == 1, (tot(0) + tot(1)) + (tot(2) + tot(3)), zero
    ).astype(BF16)

    def along_row(d):
        return remote(
            high.at[y, mine, :], high.at[y, mine, :], high_send.at[d - 1], high_recv.at[d - 1],
            device(z, row_peer(d), core),
        )

    for d in FAR_FIRST:
        along_row(d).start()

    def share_high(i, h):
        return remote(high.at[h, mine, :], high.at[h, mine, :], fwh_send.at[i], fwh_recv.at[i], sibling)

    share_high(0, y).start()

    @pl.when(core == 1)
    def _():
        to_core1.wait_recv()
        for h in range(HEADS_HERE):
            acc[h] += w_cols[h, :, 2:3] * nn(q_s[h], core0[h])

    def share_low(level):
        return remote(
            low.at[level, :, mine, :], low.at[level, :, mine, :], fwl_send.at[level], fwl_recv.at[level], sibling
        )

    conds = (y0, y1, y2)

    @pl.when(y0)
    def _():
        to_next.wait_recv()
        share_low(0).start()

    for level in (1, 2):

        @pl.when(conds[level])
        def _():
            for d in range(1, RING):
                low_copy(level, d).wait_recv()
            share_low(level).start()

    for level in range(3):

        @pl.when(conds[level])
        def _():
            share_low(level).wait_recv()
            for h in range(HEADS_HERE):
                acc[h] += w_cols[h, :, 3 + level : 4 + level] * nn(q_s[h], low[level, h])

    sq[...] = jnp.zeros_like(sq)

    def read_high(i, d):
        h = lax.rem(y + RING - d, RING)
        share_high(i, h).wait_recv()
        r = nn(q_s[h], high[h])
        a = acc[h]
        for level in range(3):
            a += w_cols[h, :, 6 + level : 7 + level] * r[:, level * 128 : (level + 1) * 128]
        acc[h] = a
        sq[...] += a * a

    arrivals = (0,) + NEAR_FIRST
    for i, d in enumerate(arrivals):
        if d:
            along_row(d).wait_recv()
            share_high(i, lax.rem(y + RING - d, RING)).start()
            read_high(i - 1, arrivals[i - 1])
    read_high(RING - 1, arrivals[RING - 1])

    sq_in[col, 0:1, :] = jnp.sum(sq[...].T, axis=0, keepdims=True)

    def to_cols(d):
        return remote(
            sq_in.at[col, 0:1], sq_in.at[col, 0:1], sq_send.at[d - 1], sq_recv.at[d - 1],
            (seq, lax.rem(col + d, COLS)),
        )

    for d in (2, 1, 3):
        to_cols(d).start()
    g_load.wait()
    for d in (1, 3, 2):
        to_cols(d).wait_recv()
    squares = (sq_in[0, 0:1, :] + sq_in[1, 0:1, :]) + (sq_in[2, 0:1, :] + sq_in[3, 0:1, :])
    inverse = lax.rsqrt(squares / D + EPSILON)
    scale = jnp.broadcast_to(inverse, (HEAD_DIM, TOK)).T

    def store(h):
        columns = pl.ds(h * HEAD_DIM, HEAD_DIM)
        return pltpu.make_async_copy(out_s.at[h], out_hbm.at[:, columns], out_sem.at[h])

    for h in range(HEADS_HERE):
        out_s[h] = (acc[h] * scale * g_v[:, h * HEAD_DIM : (h + 1) * HEAD_DIM]).astype(BF16)
        store(h).start()

    for i, d in enumerate(order):
        to_sibling(i, row_peer(d)).wait_send()

    @pl.when(core == 0)
    def _():
        to_core1.wait_send()

    @pl.when(jnp.logical_not(y0))
    def _():
        to_next.wait_send()

    for d in range(1, RING):
        to_owner(d).wait_send()
        to_column(d).wait_send()
        along_row(d).wait_send()
        target = row_peer(d)

        @pl.when(lax.rem(target // 2, 2) == 1)
        def _():
            low_copy(1, d).wait_send()

        @pl.when(target // 4 == 1)
        def _():
            low_copy(2, d).wait_send()

    for level in range(3):

        @pl.when(conds[level])
        def _():
            share_low(level).wait_send()

    for i, d in enumerate(arrivals):
        share_high(i, lax.rem(y + RING - d, RING)).wait_send()
    for d in range(1, COLS):
        to_cols(d).wait_send()
    for h in range(HEADS_HERE):
        store(h).wait()


def local(queries, keys, values, level_weights, norm_gain):
    hd, tok, half, ring = HEAD_DIM, TOK, HALF, RING
    dma = pltpu.SemaphoreType.DMA
    any_space = pl.BlockSpec(memory_space=pl.ANY)
    scratch = [
        pltpu.VMEM((8, tok, hd), BF16),
        pltpu.VMEM((8, tok, hd), BF16),
        pltpu.VMEM((8, tok, hd), BF16),
        pltpu.VMEM((9, 8, tok), F32),
        pltpu.VMEM((1, 1024), F32),
        pltpu.VMEM((8, 16, tok), F32),
        pltpu.VMEM((8, tok, 16), F32),
        pltpu.VMEM((8, tok, hd), BF16),
        pltpu.VMEM((8, hd, hd), BF16),
        pltpu.VMEM((8, hd, hd), F32),
        pltpu.VMEM((8, hd, hd), BF16),
        pltpu.VMEM((8, half, hd), F32),
        pltpu.VMEM((8, hd, hd), BF16),
        pltpu.VMEM((8, half, hd), BF16),
        pltpu.VMEM((ring, half, hd), BF16),
        pltpu.VMEM((3, half, hd), BF16),
        pltpu.VMEM((ring, half, hd), BF16),
        pltpu.VMEM((3, 8, hd, hd), BF16),
        pltpu.VMEM((8, hd, 3 * hd), BF16),
        pltpu.VMEM((8, tok, hd), F32),
        pltpu.VMEM((tok, hd), F32),
        pltpu.VMEM((COLS, 8, tok), F32),
        dma((3, 8)), dma((2,)), dma((8,)),
        dma((8,)), dma((8,)), dma, dma, dma((7,)), dma((7,)), dma, dma,
        dma((2, 7)), dma((2, 7)), dma((7,)), dma((7,)), dma((7,)), dma((7,)),
        dma((3,)), dma((3,)), dma((8,)), dma((8,)), dma((3,)), dma((3,)),
    ]
    return pl.pallas_call(
        kernel,
        out_shape=jax.ShapeDtypeStruct((tok, 8 * hd), BF16),
        in_specs=[any_space] * 5,
        out_specs=any_space,
        scratch_shapes=scratch,
        compiler_params=pltpu.CompilerParams(
            collective_id=0, has_side_effects=True, vmem_limit_bytes=40 * 1024 * 1024
        ),
        cost_estimate=pl.CostEstimate(flops=2_000_000_000, bytes_accessed=4_400_000, transcendentals=0),
    )(queries, keys, values, level_weights, norm_gain.reshape(1, -1))


def solution(mesh):
    return jax.shard_map(
        local,
        mesh=mesh,
        in_specs=(
            P("seq", "head"),
            P("seq", "head"),
            P("seq", "head"),
            P(None, "head", "seq"),
            P("head"),
        ),
        out_specs=P("seq", "head"),
        check_vma=False,
    )
```

```python
import jax
import jax.numpy as jnp
from jax import lax
from jax.experimental import pallas as pl
from jax.experimental.pallas import tpu as pltpu
from jax.sharding import PartitionSpec as P

HEAD_DIM = 128
STRETCH = 256
D = 4096
EPSILON = 1e-06

RING = 8
COLS = 4
HEADS_HERE = 8
TOK = 512
EARLY = 5
HALF = 64
FAR_FIRST = (4, 3, 5, 2, 6, 1, 7)
NEAR_FIRST = (1, 7, 2, 6, 3, 5, 4)
PAIRS = ((0, 1), (0, 2), (1, 2), (2, 3), (0, 4), (1, 4), (2, 4), (3, 4), (4, 5), (4, 6), (5, 6), (6, 7))
MESH = pl.DeviceIdType.MESH
F32 = jnp.float32
BF16 = jnp.bfloat16


def nt(a, b):
    return lax.dot_general(a, b, (((1,), (1,)), ((), ())), preferred_element_type=F32)


def tn(a, b):
    return lax.dot_general(a, b, (((0,), (0,)), ((), ())), preferred_element_type=F32)


def nn(a, b):
    return jnp.dot(a, b, preferred_element_type=F32)


def kernel(
    q_hbm, k_hbm, v_hbm, w_hbm, g_hbm, out_hbm,
    q_s, k_s, v_s, w_v, g_v, w_rows, w_cols, out_s,
    first, own_sum, own_bf, pair_in, core0, chip_sum, ring_in, ring_sum, totals, low, high,
    acc, sq, sq_in,
    load_sem, misc_sem, out_sem, ready,
    pair_send, pair_recv, core_send, core_recv, ring_send, ring_recv, next_send, next_recv,
    low_send, low_recv, tot_send, tot_recv, high_send, high_recv, up_send, up_recv,
    fwl_send, fwl_recv, fwh_send, fwh_recv, sq_send, sq_recv,
):
    seq = lax.axis_index("seq")
    col = lax.axis_index("head")
    core = lax.rem(seq, 2)
    y = lax.rem(seq // 2, RING)
    z = seq // (2 * RING)
    y_bits = (lax.rem(y, 2) == 1, lax.rem(y // 2, 2) == 1, y // 4 == 1)
    z_bits = (lax.rem(z, 2) == 1, lax.rem(z // 2, 2) == 1, z // 4 == 1)
    sent = []

    def device(z_, y_, core_):
        return (z_ * (2 * RING) + y_ * 2 + core_, col)

    sibling = device(z, y, 1 - core)
    mine = pl.ds(pl.multiple_of(core * HALF, HALF), HALF)
    other = pl.ds(pl.multiple_of((1 - core) * HALF, HALF), HALF)

    def row_peer(d):
        return lax.rem(y + d, RING)

    def remote(src, dst, send, recv, target):
        return pltpu.make_async_remote_copy(
            src_ref=src, dst_ref=dst, send_sem=send, recv_sem=recv, device_id=target, device_id_type=MESH
        )

    def when(cond, f):
        if cond is None:
            f()
        else:
            pl.when(cond)(f)

    def launch(copy, cond=None):
        when(cond, copy.start)
        sent.append((cond, copy))

    def finish():
        for cond, copy in sent:
            when(cond, copy.wait_send)

    order = FAR_FIRST + (0,)
    loads = {}
    for name, src, dst, slot in (("k", k_hbm, k_s, 0), ("v", v_hbm, v_s, 1), ("q", q_hbm, q_s, 2)):
        for i, d in enumerate(order):
            h = row_peer(d)
            columns = pl.ds(pl.multiple_of(h * HEAD_DIM, HEAD_DIM), HEAD_DIM)
            loads[name, i] = pltpu.make_async_copy(src.at[:, columns], dst.at[h], load_sem.at[slot, i])
    for i in range(HEADS_HERE):
        loads["k", i].start()
        loads["v", i].start()
    w_load = pltpu.make_async_copy(w_hbm, w_v, misc_sem.at[0])
    g_load = pltpu.make_async_copy(g_hbm, g_v, misc_sem.at[1])

    barrier = pltpu.get_barrier_semaphore()

    def greet(target):
        pl.semaphore_signal(barrier, inc=1, device_id=target, device_id_type=MESH)

    for a, b in PAIRS:
        pl.when(z == a)(lambda: greet(device(b, y, core)))
    greet(sibling)
    for d in range(1, RING):
        greet(device(z, row_peer(d), core))
    for d in range(1, COLS):
        greet((seq, lax.rem(col + d, COLS)))

    for h in range(HEADS_HERE):
        loads["q", h].start()
    w_load.start()
    g_load.start()
    for level in range(3):

        @pl.when(jnp.logical_not(z_bits[level]))
        def _():
            high[:, mine, level * 128 : (level + 1) * 128] = jnp.zeros((HEADS_HERE, HALF, HEAD_DIM), BF16)

    to_sibling = []
    for i, d in enumerate(order):
        h = row_peer(d)
        to_sibling.append(
            remote(own_sum.at[h, other, :], pair_in.at[h], pair_send.at[i], pair_recv.at[i], sibling)
        )
    for i, d in enumerate(order):
        h = row_peer(d)
        loads["k", i].wait()
        loads["v", i].wait()
        k = k_s[h]
        v = v_s[h]
        s0 = tn(k[:STRETCH], v[:STRETCH])
        s1 = tn(k[STRETCH:], v[STRETCH:])
        first[h] = s0.astype(BF16)
        s = s0 + s1
        own_sum[h] = s
        own_bf[h] = s.astype(BF16)
        if i == 0:
            for row in range(RING):
                rows_in = [a for a, b in PAIRS if b == row]

                @pl.when(z == row)
                def _():
                    pl.semaphore_wait(barrier, 1 + RING - 1 + COLS - 1 + len(rows_in))
                    for a in rows_in:
                        pl.semaphore_signal(
                            ready.at[row], inc=1, device_id=device(a, y, core), device_id_type=MESH
                        )

        launch(to_sibling[i])

    to_core1 = remote(own_bf, core0, core_send, core_recv, sibling)
    launch(to_core1, core == 0)

    def to_owner(d):
        h = row_peer(d)
        return remote(chip_sum.at[h], ring_in.at[y], ring_send.at[d - 1], ring_recv.at[d - 1], device(z, h, core))

    for i, d in enumerate(order):
        h = row_peer(d)
        to_sibling[i].wait_recv()
        c = (own_sum[h, mine, :] + pair_in[h]).astype(BF16)
        chip_sum[h] = c
        if d:
            launch(to_owner(d))
        else:
            ring_in[y] = c

    w_load.wait()
    for h in range(HEADS_HERE):
        for level in range(9):
            w_rows[h, level : level + 1, :] = w_v[level, h : h + 1, :]
        w_rows[h, 9:16, :] = jnp.zeros((7, TOK), F32)
    for h in range(HEADS_HERE):
        w_cols[h] = w_rows[h].T

    for h in range(HEADS_HERE):
        loads["q", h].wait()

    causal = lax.broadcasted_iota(jnp.int32, (STRETCH, STRETCH), 0) >= lax.broadcasted_iota(
        jnp.int32, (STRETCH, STRETCH), 1
    )

    def within(h):
        for s in range(2):
            rows = slice(s * STRETCH, (s + 1) * STRETCH)
            qs = q_s[h, rows, :]
            probs = jnp.where(causal, nt(qs, k_s[h, rows, :]), 0.0).astype(BF16)
            part = w_cols[h, rows, 0:1] * nn(probs, v_s[h, rows, :])
            if s == 1:
                part += w_cols[h, rows, 1:2] * nn(qs, first[h])
            acc[h, rows, :] = part

    for h in range(0, EARLY):
        within(h)

    to_next = remote(
        chip_sum, low.at[0, :, mine, :], next_send, next_recv, device(z, lax.rem(y + 1, RING), core)
    )
    launch(to_next, jnp.logical_not(y_bits[0]))

    for d in range(1, RING):
        to_owner(d).wait_recv()
    part = [ring_in[j].astype(F32) for j in range(RING)]
    s01 = part[0] + part[1]
    s0123 = s01 + (part[2] + part[3])
    s45 = part[4] + part[5]
    totals[z] = s0123 + (s45 + (part[6] + part[7]))

    for a, b in PAIRS:

        @pl.when(z == a)
        def _():
            pl.semaphore_wait(ready.at[b], 1)

        launch(
            remote(totals.at[a], totals.at[a], tot_send.at[b], tot_recv.at[a], device(b, y, core)), z == a
        )

    ring_sum[0] = s01.astype(BF16)
    ring_sum[1] = s45.astype(BF16)
    ring_sum[2] = s0123.astype(BF16)

    for h in range(EARLY, HEADS_HERE):
        within(h)

    level_lanes = [slice(level * 128, (level + 1) * 128) for level in range(3)]
    for row in range(1, RING):
        rows_in = [a for a, b in PAIRS if b == row]
        level = len(rows_in).bit_length() - 1

        @pl.when(z == row)
        def _():
            for a in rows_in:
                remote(totals.at[a], totals.at[a], tot_send.at[row], tot_recv.at[a], device(row, y, core)).wait_recv()
            state = totals[rows_in[0]]
            for a in rows_in[1:]:
                state = state + totals[a]
            high[y, mine, level_lanes[level]] = state.astype(BF16)

    lowest = (1 - lax.rem(z, 2)) * (2 - lax.rem(z // 2, 2))
    lanes = pl.ds(pl.multiple_of(lowest * 128, 128), 128)

    def along_row(d):
        return remote(
            high.at[y, mine, lanes], high.at[y, mine, lanes], high_send.at[d - 1], high_recv.at[d - 1],
            device(z, row_peer(d), core),
        )

    for d in FAR_FIRST:
        launch(along_row(d), z > 0)

    def low_copy(level, d):
        target = row_peer(d)
        src = ring_sum.at[target // 4] if level == 1 else ring_sum.at[2]
        return remote(
            src, low.at[level, y, mine, :], low_send.at[level - 1, d - 1], low_recv.at[level - 1, d - 1],
            device(z, target, core),
        )

    for d in FAR_FIRST:
        target = row_peer(d)
        launch(low_copy(1, d), lax.rem(target // 2, 2) == 1)
        launch(low_copy(2, d), target // 4 == 1)

    @pl.when(y_bits[1])
    def _():
        low[1, y, mine, :] = ring_sum[y // 4]

    @pl.when(y_bits[2])
    def _():
        low[2, y, mine, :] = ring_sum[2]

    @pl.when(core == 1)
    def _():
        to_core1.wait_recv()
        for h in range(HEADS_HERE):
            acc[h] += w_cols[h, :, 2:3] * nn(q_s[h], core0[h])

    def share_low(level):
        return remote(
            low.at[level, :, mine, :], low.at[level, :, mine, :], fwl_send.at[level], fwl_recv.at[level], sibling
        )

    def low_arrivals():
        for level in range(3):

            @pl.when(y_bits[level])
            def _():
                if level == 0:
                    to_next.wait_recv()
                else:
                    for d in range(1, RING):
                        low_copy(level, d).wait_recv()
                share_low(level).start()

        for level in range(3):

            @pl.when(y_bits[level])
            def _():
                share_low(level).wait_recv()
                for h in range(HEADS_HERE):
                    acc[h] += w_cols[h, :, 3 + level : 4 + level] * nn(q_s[h], low[level, h])

    for level in range(3):
        sent.append((y_bits[level], share_low(level)))

    pl.when(z == RING - 1)(low_arrivals)

    def share_high(i, h):
        return remote(high.at[h, mine, :], high.at[h, mine, :], fwh_send.at[i], fwh_recv.at[i], sibling)

    def upward(level, i, h):
        ref = high.at[h, mine, level_lanes[level]]
        return remote(ref, ref, up_send.at[level - 1, i], up_recv.at[level - 1, i], device(lax.rem(z + 1, RING), y, core))

    arrivals = (0,) + NEAR_FIRST
    from_below = {1: lax.rem(z, 4) == 3, 2: z > 4}
    go_up = {1: lax.rem(z, 4) == 2, 2: jnp.logical_and(z >= 4, z < 7)}
    for i, d in enumerate(arrivals):
        h = lax.rem(y + RING - d, RING)
        for level in (2, 1):
            pl.when(from_below[level])(upward(level, i, h).wait_recv)
        if d:
            pl.when(z > 0)(along_row(d).wait_recv)
        for level in (2, 1):
            launch(upward(level, i, h), go_up[level])
        launch(share_high(i, h))

    pl.when(z < RING - 1)(low_arrivals)

    sq[...] = jnp.zeros_like(sq)
    for i, d in enumerate(arrivals):
        h = lax.rem(y + RING - d, RING)
        share_high(i, h).wait_recv()
        r = nn(q_s[h], high[h])
        a = acc[h]
        for level in range(3):
            a += w_cols[h, :, 6 + level : 7 + level] * r[:, level_lanes[level]]
        acc[h] = a
        sq[...] += a * a

    sq_in[col, 0:1, :] = jnp.sum(sq[...].T, axis=0, keepdims=True)

    def to_cols(d):
        return remote(
            sq_in.at[col, 0:1], sq_in.at[col, 0:1], sq_send.at[d - 1], sq_recv.at[d - 1],
            (seq, lax.rem(col + d, COLS)),
        )

    for d in (2, 1, 3):
        launch(to_cols(d))
    g_load.wait()
    for d in (1, 3, 2):
        to_cols(d).wait_recv()
    squares = (sq_in[0, 0:1, :] + sq_in[1, 0:1, :]) + (sq_in[2, 0:1, :] + sq_in[3, 0:1, :])
    inverse = lax.rsqrt(squares / D + EPSILON)
    scale = jnp.broadcast_to(inverse, (HEAD_DIM, TOK)).T

    def store(h):
        columns = pl.ds(h * HEAD_DIM, HEAD_DIM)
        return pltpu.make_async_copy(out_s.at[h], out_hbm.at[:, columns], out_sem.at[h])

    for h in range(HEADS_HERE):
        out_s[h] = (acc[h] * scale * g_v[:, h * HEAD_DIM : (h + 1) * HEAD_DIM]).astype(BF16)
        store(h).start()
    finish()
    for h in range(HEADS_HERE):
        store(h).wait()


def local(queries, keys, values, level_weights, norm_gain):
    hd, tok, half, ring = HEAD_DIM, TOK, HALF, RING
    dma = pltpu.SemaphoreType.DMA
    any_space = pl.BlockSpec(memory_space=pl.ANY)
    scratch = [
        pltpu.VMEM((8, tok, hd), BF16),
        pltpu.VMEM((8, tok, hd), BF16),
        pltpu.VMEM((8, tok, hd), BF16),
        pltpu.VMEM((9, 8, tok), F32),
        pltpu.VMEM((1, 1024), F32),
        pltpu.VMEM((8, 16, tok), F32),
        pltpu.VMEM((8, tok, 16), F32),
        pltpu.VMEM((8, tok, hd), BF16),
        pltpu.VMEM((8, hd, hd), BF16),
        pltpu.VMEM((8, hd, hd), F32),
        pltpu.VMEM((8, hd, hd), BF16),
        pltpu.VMEM((8, half, hd), F32),
        pltpu.VMEM((8, hd, hd), BF16),
        pltpu.VMEM((8, half, hd), BF16),
        pltpu.VMEM((ring, half, hd), BF16),
        pltpu.VMEM((3, half, hd), BF16),
        pltpu.VMEM((ring, half, hd), F32),
        pltpu.VMEM((3, 8, hd, hd), BF16),
        pltpu.VMEM((8, hd, 3 * hd), BF16),
        pltpu.VMEM((8, tok, hd), F32),
        pltpu.VMEM((tok, hd), F32),
        pltpu.VMEM((COLS, 8, tok), F32),
        dma((3, 8)), dma((2,)), dma((8,)), pltpu.SemaphoreType.REGULAR((8,)),
        dma((8,)), dma((8,)), dma, dma, dma((7,)), dma((7,)), dma, dma,
        dma((2, 7)), dma((2, 7)), dma((8,)), dma((8,)), dma((7,)), dma((7,)), dma((2, 8)), dma((2, 8)),
        dma((3,)), dma((3,)), dma((8,)), dma((8,)), dma((3,)), dma((3,)),
    ]
    return pl.pallas_call(
        kernel,
        out_shape=jax.ShapeDtypeStruct((tok, 8 * hd), BF16),
        in_specs=[any_space] * 5,
        out_specs=any_space,
        scratch_shapes=scratch,
        compiler_params=pltpu.CompilerParams(
            collective_id=0, has_side_effects=True, vmem_limit_bytes=60 * 1024 * 1024
        ),
        cost_estimate=pl.CostEstimate(flops=2_000_000_000, bytes_accessed=4_400_000, transcendentals=0),
    )(queries, keys, values, level_weights, norm_gain.reshape(1, -1))


def solution(mesh):
    return jax.shard_map(
        local,
        mesh=mesh,
        in_specs=(
            P("seq", "head"),
            P("seq", "head"),
            P("seq", "head"),
            P(None, "head", "seq"),
            P("head"),
        ),
        out_specs=P("seq", "head"),
        check_vma=False,
    )
```

```python
import jax
import jax.numpy as jnp
from jax import lax
from jax.experimental import pallas as pl
from jax.experimental.pallas import tpu as pltpu
from jax.sharding import PartitionSpec as P

HEAD_DIM = 128
STRETCH = 256
D = 4096
EPSILON = 1e-06

RING = 8
COLS = 4
HEADS_HERE = 8
TOK = 512
EARLY = 5
HALF = 64
FAR_FIRST = (4, 3, 5, 2, 6, 1, 7)
NEAR_FIRST = (1, 7, 2, 6, 3, 5, 4)
PAIRS = ((0, 1), (0, 2), (1, 2), (2, 3), (0, 4), (1, 4), (2, 4), (3, 4), (4, 5), (4, 6), (5, 6), (6, 7))
TARGETS = {a: [b for c, b in PAIRS if c == a] for a in range(RING - 1)}
MESH = pl.DeviceIdType.MESH
F32 = jnp.float32
BF16 = jnp.bfloat16


def nt(a, b):
    return lax.dot_general(a, b, (((1,), (1,)), ((), ())), preferred_element_type=F32)


def tn(a, b):
    return lax.dot_general(a, b, (((0,), (0,)), ((), ())), preferred_element_type=F32)


def nn(a, b):
    return jnp.dot(a, b, preferred_element_type=F32)


def kernel(
    q_hbm, k_hbm, v_hbm, w_hbm, g_hbm, out,
    q_s, kv_s, w_v, g_v, w_rows, w_cols,
    first, own_sum, own_bf, pair_in, core0, chip_sum, ring_in, ring_sum, totals, low, high,
    acc, sq, sq_in,
    load_sem, misc_sem, ready,
    pair_send, pair_recv, core_send, core_recv, ring_send, ring_recv, next_send, next_recv,
    low_send, low_recv, tot_send, tot_recv, high_send, high_recv, up_send, up_recv,
    fwl_send, fwl_recv, fwh_send, fwh_recv, sq_send, sq_recv,
):
    seq = lax.axis_index("seq")
    col = lax.axis_index("head")
    core = lax.rem(seq, 2)
    y = lax.rem(seq // 2, RING)
    z = seq // (2 * RING)
    y_bits = (lax.rem(y, 2) == 1, lax.rem(y // 2, 2) == 1, y // 4 == 1)
    z_bits = (lax.rem(z, 2) == 1, lax.rem(z // 2, 2) == 1, z // 4 == 1)
    ends = []

    def device(z_, y_, core_):
        return (z_ * (2 * RING) + y_ * 2 + core_, col)

    sibling = device(z, y, 1 - core)
    mine = pl.ds(pl.multiple_of(core * HALF, HALF), HALF)
    other = pl.ds(pl.multiple_of((1 - core) * HALF, HALF), HALF)

    def row_peer(d):
        return lax.rem(y + d, RING)

    def remote(src, dst, send, recv, target):
        return pltpu.make_async_remote_copy(
            src_ref=src, dst_ref=dst, send_sem=send, recv_sem=recv, device_id=target, device_id_type=MESH
        )

    def when(cond, f):
        if cond is None:
            f()
        else:
            pl.when(cond)(f)

    def launch(copy, cond=None, alone=True):
        when(cond, copy.start)
        if alone:
            ends.append((cond, copy))

    def finish():
        for cond, copy in ends:
            when(cond, copy.wait_send)

    order = FAR_FIRST + (0,)

    def columns_of(i):
        return pl.ds(pl.multiple_of(row_peer(order[i]) * HEAD_DIM, HEAD_DIM), HEAD_DIM)

    for i, d in enumerate(order):
        pltpu.make_async_copy(k_hbm.at[:, columns_of(i)], kv_s.at[row_peer(d), 0], load_sem.at[i]).start()
        pltpu.make_async_copy(v_hbm.at[:, columns_of(i)], kv_s.at[row_peer(d), 1], load_sem.at[i]).start()
    w_load = pltpu.make_async_copy(w_hbm, w_v, misc_sem.at[0])
    g_load = pltpu.make_async_copy(g_hbm, g_v, misc_sem.at[1])

    barrier = pltpu.get_barrier_semaphore()

    def greet(target):
        pl.semaphore_signal(barrier, inc=1, device_id=target, device_id_type=MESH)

    for d in FAR_FIRST:
        greet(device(z, row_peer(d), core))
    for a, b in PAIRS:
        pl.when(z == a)(lambda: greet(device(b, y, core)))
    greet(sibling)
    for d in range(1, COLS):
        greet((seq, lax.rem(col + d, COLS)))

    for i, d in enumerate(order):
        pltpu.make_async_copy(q_hbm.at[:, columns_of(i)], q_s.at[row_peer(d)], misc_sem.at[2]).start()
    w_load.start()
    g_load.start()
    for level in range(3):

        @pl.when(jnp.logical_not(z_bits[level]))
        def _():
            high[:, mine, level * 128 : (level + 1) * 128] = jnp.zeros((HEADS_HERE, HALF, HEAD_DIM), BF16)

    to_sibling = []
    for i, d in enumerate(order):
        h = row_peer(d)
        to_sibling.append(
            remote(own_sum.at[h, other, :], pair_in.at[h], pair_send, pair_recv.at[i], sibling)
        )
    for i, d in enumerate(order):
        h = row_peer(d)
        pltpu.make_async_copy(kv_s.at[h], kv_s.at[h], load_sem.at[i]).wait()
        k = kv_s[h, 0]
        v = kv_s[h, 1]
        s0 = tn(k[:STRETCH], v[:STRETCH])
        s1 = tn(k[STRETCH:], v[STRETCH:])
        first[h] = s0.astype(BF16)
        s = s0 + s1
        own_sum[h] = s
        own_bf[h] = s.astype(BF16)
        if i == 0:
            for row in range(RING):
                rows_in = [a for a, b in PAIRS if b == row]

                @pl.when(z == row)
                def _():
                    pl.semaphore_wait(barrier, 1 + RING - 1 + COLS - 1 + len(rows_in))
                    for a in rows_in:
                        pl.semaphore_signal(
                            ready.at[TARGETS[a].index(row)], inc=1, device_id=device(a, y, core), device_id_type=MESH
                        )

        launch(to_sibling[i], alone=False)

    ends.append((None, remote(own_sum.at[:, other, :], pair_in, pair_send, pair_recv.at[0], sibling)))
    to_core1 = remote(own_bf, core0, core_send, core_recv, sibling)
    launch(to_core1, core == 0)

    def to_owner(d):
        h = row_peer(d)
        return remote(chip_sum.at[h], ring_in.at[y], ring_send, ring_recv, device(z, h, core))

    for i, d in enumerate(order):
        h = row_peer(d)
        to_sibling[i].wait_recv()
        c = (own_sum[h, mine, :] + pair_in[h]).astype(BF16)
        chip_sum[h] = c
        if d:
            launch(to_owner(d), alone=False)
        else:
            ring_in[y] = c

    def row_total(count, send, recv):
        return remote(chip_sum.at[0:count], ring_in.at[0:count], send, recv, device(z, row_peer(1), core))

    from_row = row_total(RING - 1, ring_send, ring_recv)
    ends.append((None, from_row))

    w_load.wait()
    for h in range(HEADS_HERE):
        for level in range(9):
            w_rows[h, level : level + 1, :] = w_v[level, h : h + 1, :]
        w_rows[h, 9:16, :] = jnp.zeros((7, TOK), F32)
    for h in range(HEADS_HERE):
        w_cols[h] = w_rows[h].T

    pltpu.make_async_copy(q_s, q_s, misc_sem.at[2]).wait()

    causal = lax.broadcasted_iota(jnp.int32, (STRETCH, STRETCH), 0) >= lax.broadcasted_iota(
        jnp.int32, (STRETCH, STRETCH), 1
    )

    def within(h):
        for s in range(2):
            rows = slice(s * STRETCH, (s + 1) * STRETCH)
            qs = q_s[h, rows, :]
            probs = jnp.where(causal, nt(qs, kv_s[h, 0, rows, :]), 0.0).astype(BF16)
            part = w_cols[h, rows, 0:1] * nn(probs, kv_s[h, 1, rows, :])
            if s == 1:
                part += w_cols[h, rows, 1:2] * nn(qs, first[h])
            acc[h, rows, :] = part

    for h in range(0, EARLY):
        within(h)

    to_next = remote(
        chip_sum, low.at[0, :, mine, :], next_send, next_recv, device(z, lax.rem(y + 1, RING), core)
    )
    launch(to_next, jnp.logical_not(y_bits[0]))

    from_row.wait_recv()
    part = [ring_in[j].astype(F32) for j in range(RING)]
    s01 = part[0] + part[1]
    s0123 = s01 + (part[2] + part[3])
    s45 = part[4] + part[5]
    totals[z] = s0123 + (s45 + (part[6] + part[7]))

    for a, b in PAIRS:

        @pl.when(z == a)
        def _():
            pl.semaphore_wait(ready.at[TARGETS[a].index(b)], 1)

        launch(
            remote(
                totals.at[a], totals.at[a], tot_send.at[TARGETS[a].index(b)],
                tot_recv.at[a - b + (b & -b)], device(b, y, core),
            ),
            z == a,
        )

    ring_sum[0] = s01.astype(BF16)
    ring_sum[1] = s45.astype(BF16)
    ring_sum[2] = s0123.astype(BF16)

    def low_copy(level, d):
        target = row_peer(d)
        src = ring_sum.at[target // 4] if level == 1 else ring_sum.at[2]
        return remote(
            src, low.at[level, y, mine, :], low_send.at[level - 1], low_recv.at[level - 1], device(z, target, core)
        )

    for d in FAR_FIRST:
        launch(low_copy(1, d), lax.rem(row_peer(d) // 2, 2) == 1, alone=False)
    for level in (1, 2):
        ends.append((y_bits[level], row_total(3, low_send.at[level - 1], ring_recv)))
        ends.append((jnp.logical_not(y_bits[level]), row_total(4, low_send.at[level - 1], ring_recv)))

    @pl.when(y_bits[1])
    def _():
        low[1, y, mine, :] = ring_sum[y // 4]

    @pl.when(y_bits[2])
    def _():
        low[2, y, mine, :] = ring_sum[2]

    for h in range(EARLY, HEADS_HERE):
        within(h)

    level_lanes = [slice(level * 128, (level + 1) * 128) for level in range(3)]
    for row in range(1, RING):
        rows_in = [a for a, b in PAIRS if b == row]
        level = len(rows_in).bit_length() - 1

        @pl.when(z == row)
        def _():
            for a in rows_in:
                remote(
                    totals.at[a], totals.at[a], tot_send.at[0], tot_recv.at[a - rows_in[0]], device(a, y, core)
                ).wait_recv()
            state = totals[rows_in[0]]
            for a in rows_in[1:]:
                state = state + totals[a]
            high[y, mine, level_lanes[level]] = state.astype(BF16)

    lowest = (1 - lax.rem(z, 2)) * (2 - lax.rem(z // 2, 2))
    lanes = pl.ds(pl.multiple_of(lowest * 128, 128), 128)

    def along_row(d):
        return remote(
            high.at[y, mine, lanes], high.at[y, mine, lanes], high_send, high_recv.at[d - 1],
            device(z, row_peer(d), core),
        )

    for d in FAR_FIRST:
        launch(along_row(d), z > 0, alone=False)

    @pl.when(core == 1)
    def _():
        to_core1.wait_recv()
        for h in range(HEADS_HERE):
            acc[h] += w_cols[h, :, 2:3] * nn(q_s[h], core0[h])

    when(z > 0, row_total(RING - 1, high_send, ring_recv).wait_send)
    for d in FAR_FIRST:
        launch(low_copy(2, d), row_peer(d) // 4 == 1, alone=False)

    def share_low(level):
        return remote(
            low.at[level, :, mine, :], low.at[level, :, mine, :], fwl_send.at[level], fwl_recv.at[level], sibling
        )

    def low_arrivals():
        for level in range(3):

            @pl.when(y_bits[level])
            def _():
                if level == 0:
                    to_next.wait_recv()
                else:
                    row_total(RING - 1, ring_send, low_recv.at[level - 1]).wait_recv()
                share_low(level).start()

        for level in range(3):

            @pl.when(y_bits[level])
            def _():
                share_low(level).wait_recv()
                for h in range(HEADS_HERE):
                    acc[h] += w_cols[h, :, 3 + level : 4 + level] * nn(q_s[h], low[level, h])

    for level in range(3):
        ends.append((y_bits[level], share_low(level)))

    pl.when(z == RING - 1)(low_arrivals)

    def share_high(i, h):
        return remote(high.at[h, mine, :], high.at[h, mine, :], fwh_send, fwh_recv.at[i], sibling)

    def upward(level, i, h):
        ref = high.at[h, mine, level_lanes[level]]
        return remote(ref, ref, up_send.at[level - 1], up_recv.at[level - 1, i], device(lax.rem(z + 1, RING), y, core))

    arrivals = (0,) + NEAR_FIRST
    from_below = {1: lax.rem(z, 4) == 3, 2: z > 4}
    go_up = {1: lax.rem(z, 4) == 2, 2: jnp.logical_and(z >= 4, z < 7)}
    for i, d in enumerate(arrivals):
        h = lax.rem(y + RING - d, RING)
        for level in (2, 1):
            pl.when(from_below[level])(upward(level, i, h).wait_recv)
        if d:
            pl.when(z > 0)(along_row(d).wait_recv)
        for level in (2, 1):
            launch(upward(level, i, h), go_up[level], alone=False)
        launch(share_high(i, h), alone=False)

    whole = high.at[:, mine, :]
    ends.append((None, remote(whole, whole, fwh_send, fwh_recv.at[0], sibling)))
    for level in (1, 2):
        ends.append((go_up[level], row_total(RING, up_send.at[level - 1], ring_recv)))
    pl.when(z < RING - 1)(low_arrivals)

    sq[...] = jnp.zeros_like(sq)
    for i, d in enumerate(arrivals):
        h = lax.rem(y + RING - d, RING)
        share_high(i, h).wait_recv()
        r = nn(q_s[h], high[h])
        a = acc[h]
        for level in range(3):
            a += w_cols[h, :, 6 + level : 7 + level] * r[:, level_lanes[level]]
        acc[h] = a
        sq[...] += a * a

    sq_in[col, 0:1, :] = jnp.sum(sq[...].T, axis=0, keepdims=True)

    def to_cols(d):
        return remote(
            sq_in.at[col, 0:1], sq_in.at[col, 0:1], sq_send, sq_recv,
            (seq, lax.rem(col + d, COLS)),
        )

    for d in (2, 1, 3):
        launch(to_cols(d), alone=False)
    g_load.wait()
    others = sq_in.at[0 : COLS - 1, 0:1]
    from_cols = remote(others, others, sq_send, sq_recv, (seq, lax.rem(col + 1, COLS)))
    ends.append((None, from_cols))
    from_cols.wait_recv()
    squares = (sq_in[0, 0:1, :] + sq_in[1, 0:1, :]) + (sq_in[2, 0:1, :] + sq_in[3, 0:1, :])
    inverse = lax.rsqrt(squares / D + EPSILON)
    scale = jnp.broadcast_to(inverse, (HEAD_DIM, TOK)).T

    for h in range(HEADS_HERE):
        columns = slice(h * HEAD_DIM, (h + 1) * HEAD_DIM)
        out[:, columns] = (acc[h] * scale * g_v[:, columns]).astype(BF16)
    finish()


def local(queries, keys, values, level_weights, norm_gain):
    hd, tok, half, ring = HEAD_DIM, TOK, HALF, RING
    dma = pltpu.SemaphoreType.DMA
    any_space = pl.BlockSpec(memory_space=pl.ANY)
    scratch = [
        pltpu.VMEM((8, tok, hd), BF16),
        pltpu.VMEM((8, 2, tok, hd), BF16),
        pltpu.VMEM((9, 8, tok), F32),
        pltpu.VMEM((1, 1024), F32),
        pltpu.VMEM((8, 16, tok), F32),
        pltpu.VMEM((8, tok, 16), F32),
        pltpu.VMEM((8, hd, hd), BF16),
        pltpu.VMEM((8, hd, hd), F32),
        pltpu.VMEM((8, hd, hd), BF16),
        pltpu.VMEM((8, half, hd), F32),
        pltpu.VMEM((8, hd, hd), BF16),
        pltpu.VMEM((8, half, hd), BF16),
        pltpu.VMEM((ring, half, hd), BF16),
        pltpu.VMEM((3, half, hd), BF16),
        pltpu.VMEM((ring, half, hd), F32),
        pltpu.VMEM((3, 8, hd, hd), BF16),
        pltpu.VMEM((8, hd, 3 * hd), BF16),
        pltpu.VMEM((8, tok, hd), F32),
        pltpu.VMEM((tok, hd), F32),
        pltpu.VMEM((COLS, 8, tok), F32),
        dma((8,)), dma((3,)), pltpu.SemaphoreType.REGULAR((3,)),
        dma, dma((8,)), dma, dma, dma, dma, dma, dma,
        dma((2,)), dma((2,)), dma((3,)), dma((4,)), dma, dma((7,)), dma((2,)), dma((2, 8)),
        dma((3,)), dma((3,)), dma, dma((8,)), dma, dma,
    ]
    return pl.pallas_call(
        kernel,
        out_shape=pltpu.VMEM((tok, 8 * hd), BF16),
        in_specs=[any_space] * 5,
        out_specs=pl.BlockSpec(memory_space=pltpu.VMEM),
        scratch_shapes=scratch,
        compiler_params=pltpu.CompilerParams(
            collective_id=0, has_side_effects=True, vmem_limit_bytes=60 * 1024 * 1024
        ),
        cost_estimate=pl.CostEstimate(flops=2_000_000_000, bytes_accessed=4_400_000, transcendentals=0),
    )(queries, keys, values, level_weights, norm_gain.reshape(1, -1))


def solution(mesh):
    return jax.shard_map(
        local,
        mesh=mesh,
        in_specs=(
            P("seq", "head"),
            P("seq", "head"),
            P("seq", "head"),
            P(None, "head", "seq"),
            P("head"),
        ),
        out_specs=P("seq", "head"),
        check_vma=False,
    )
```

```python
import jax
import jax.numpy as jnp
from jax import lax
from jax.experimental import pallas as pl
from jax.experimental.pallas import tpu as pltpu
from jax.sharding import PartitionSpec as P

HEAD_DIM = 128
STRETCH = 256
D = 4096
EPSILON = 1e-06

RING = 8
COLS = 4
HEADS_HERE = 8
TOK = 512
EARLY = 5
HALF = 64
FAR_FIRST = (4, 3, 5, 2, 6, 1, 7)
NEAR_FIRST = (1, 7, 2, 6, 3, 5, 4)
PAIRS = ((0, 1), (0, 2), (1, 2), (2, 3), (0, 4), (1, 4), (2, 4), (3, 4), (4, 5), (4, 6), (5, 6), (6, 7))
TO_FIRST = (1, 2, 3)
FORWARD = PAIRS + ((0, 7),)
GREET = FORWARD + ((0, 3),)
TARGETS = {a: [b for c, b in FORWARD if c == a] for a in range(RING - 1)}
MESH = pl.DeviceIdType.MESH
F32 = jnp.float32
BF16 = jnp.bfloat16


def nt(a, b):
    return lax.dot_general(a, b, (((1,), (1,)), ((), ())), preferred_element_type=F32)


def tn(a, b):
    return lax.dot_general(a, b, (((0,), (0,)), ((), ())), preferred_element_type=F32)


def nn(a, b):
    return jnp.dot(a, b, preferred_element_type=F32)


def kernel(
    q_hbm, k_hbm, v_hbm, w_hbm, g_hbm, out,
    q_s, kv_s, w_v, g_v, w_rows, w_cols,
    first, own_sum, own_bf, pair_in, core0, chip_sum, ring_in, ring_sum, totals, low, high,
    acc, sq, sq_in,
    load_sem, misc_sem, ready,
    pair_send, pair_recv, core_send, core_recv, ring_send, ring_recv, next_send, next_recv,
    low_send, low_recv, tot_send, tot_recv, high_send, high_recv, up_send, up_recv,
    fwl_send, fwl_recv, fwh_send, fwh_recv, sq_send, sq_recv,
):
    seq = lax.axis_index("seq")
    col = lax.axis_index("head")
    core = lax.rem(seq, 2)
    y = lax.rem(seq // 2, RING)
    z = seq // (2 * RING)
    y_bits = (lax.rem(y, 2) == 1, lax.rem(y // 2, 2) == 1, y // 4 == 1)
    z_bits = (lax.rem(z, 2) == 1, lax.rem(z // 2, 2) == 1, z // 4 == 1)
    ends = []

    def device(z_, y_, core_):
        return (z_ * (2 * RING) + y_ * 2 + core_, col)

    sibling = device(z, y, 1 - core)
    mine = pl.ds(pl.multiple_of(core * HALF, HALF), HALF)
    other = pl.ds(pl.multiple_of((1 - core) * HALF, HALF), HALF)

    def row_peer(d):
        return lax.rem(y + d, RING)

    def remote(src, dst, send, recv, target):
        return pltpu.make_async_remote_copy(
            src_ref=src, dst_ref=dst, send_sem=send, recv_sem=recv, device_id=target, device_id_type=MESH
        )

    def when(cond, f):
        if cond is None:
            f()
        else:
            pl.when(cond)(f)

    def launch(copy, cond=None, alone=True):
        when(cond, copy.start)
        if alone:
            ends.append((cond, copy))

    def finish():
        for cond, copy in ends:
            when(cond, copy.wait_send)

    order = FAR_FIRST + (0,)

    def columns_of(i):
        return pl.ds(pl.multiple_of(row_peer(order[i]) * HEAD_DIM, HEAD_DIM), HEAD_DIM)

    for i, d in enumerate(order):
        pltpu.make_async_copy(k_hbm.at[:, columns_of(i)], kv_s.at[row_peer(d), 0], load_sem.at[i]).start()
        pltpu.make_async_copy(v_hbm.at[:, columns_of(i)], kv_s.at[row_peer(d), 1], load_sem.at[i]).start()
    w_load = pltpu.make_async_copy(w_hbm, w_v, misc_sem.at[0])
    g_load = pltpu.make_async_copy(g_hbm, g_v, misc_sem.at[1])

    barrier = pltpu.get_barrier_semaphore()

    def greet(target):
        pl.semaphore_signal(barrier, inc=1, device_id=target, device_id_type=MESH)

    for d in FAR_FIRST:
        greet(device(z, row_peer(d), core))
    for a, b in GREET:
        pl.when(z == a)(lambda: greet(device(b, y, core)))
    greet(sibling)
    for d in range(1, COLS):
        greet((seq, lax.rem(col + d, COLS)))

    for i, d in enumerate(order):
        pltpu.make_async_copy(q_hbm.at[:, columns_of(i)], q_s.at[row_peer(d)], misc_sem.at[2]).start()
    w_load.start()
    g_load.start()
    for level in range(3):

        @pl.when(jnp.logical_and(jnp.logical_not(z_bits[level]), z > 0))
        def _():
            high[:, mine, level * 128 : (level + 1) * 128] = jnp.zeros((HEADS_HERE, HALF, HEAD_DIM), BF16)

    to_sibling = []
    for i, d in enumerate(order):
        h = row_peer(d)
        to_sibling.append(
            remote(own_sum.at[h, other, :], pair_in.at[h], pair_send, pair_recv.at[i], sibling)
        )
    for i, d in enumerate(order):
        h = row_peer(d)
        pltpu.make_async_copy(kv_s.at[h], kv_s.at[h], load_sem.at[i]).wait()
        k = kv_s[h, 0]
        v = kv_s[h, 1]
        s0 = tn(k[:STRETCH], v[:STRETCH])
        s1 = tn(k[STRETCH:], v[STRETCH:])
        first[h] = s0.astype(BF16)
        s = s0 + s1
        own_sum[h] = s
        own_bf[h] = s.astype(BF16)
        if i == 0:
            for row in range(RING):
                greeted = [a for a, b in GREET if b == row]

                @pl.when(z == row)
                def _():
                    pl.semaphore_wait(barrier, 1 + RING - 1 + COLS - 1 + len(greeted))
                    for a in [a for a, b in FORWARD if b == row]:
                        pl.semaphore_signal(
                            ready.at[TARGETS[a].index(row)], inc=1, device_id=device(a, y, core), device_id_type=MESH
                        )

        launch(to_sibling[i], alone=False)

    ends.append((None, remote(own_sum.at[:, other, :], pair_in, pair_send, pair_recv.at[0], sibling)))
    to_core1 = remote(own_bf, core0, core_send, core_recv, sibling)
    launch(to_core1, core == 0)

    def to_owner(d):
        h = row_peer(d)
        return remote(chip_sum.at[h], ring_in.at[y], ring_send, ring_recv, device(z, h, core))

    for i, d in enumerate(order):
        h = row_peer(d)
        to_sibling[i].wait_recv()
        c = (own_sum[h, mine, :] + pair_in[h]).astype(BF16)
        chip_sum[h] = c
        if d:
            launch(to_owner(d), alone=False)
        else:
            ring_in[y] = c

    def row_total(count, send, recv):
        return remote(chip_sum.at[0:count], ring_in.at[0:count], send, recv, device(z, row_peer(1), core))

    from_row = row_total(RING - 1, ring_send, ring_recv)
    ends.append((None, from_row))

    w_load.wait()
    for h in range(HEADS_HERE):
        for level in range(9):
            w_rows[h, level : level + 1, :] = w_v[level, h : h + 1, :]
        w_rows[h, 9:16, :] = jnp.zeros((7, TOK), F32)
    for h in range(HEADS_HERE):
        w_cols[h] = w_rows[h].T

    pltpu.make_async_copy(q_s, q_s, misc_sem.at[2]).wait()

    causal = lax.broadcasted_iota(jnp.int32, (STRETCH, STRETCH), 0) >= lax.broadcasted_iota(
        jnp.int32, (STRETCH, STRETCH), 1
    )

    def within(h):
        for s in range(2):
            rows = slice(s * STRETCH, (s + 1) * STRETCH)
            qs = q_s[h, rows, :]
            probs = jnp.where(causal, nt(qs, kv_s[h, 0, rows, :]), 0.0).astype(BF16)
            part = w_cols[h, rows, 0:1] * nn(probs, kv_s[h, 1, rows, :])
            if s == 1:
                part += w_cols[h, rows, 1:2] * nn(qs, first[h])
            acc[h, rows, :] = part

    for h in range(0, EARLY):
        within(h)

    to_next = remote(
        chip_sum, low.at[0, :, mine, :], next_send, next_recv, device(z, lax.rem(y + 1, RING), core)
    )
    launch(to_next, jnp.logical_not(y_bits[0]))

    from_row.wait_recv()
    part = [ring_in[j].astype(F32) for j in range(RING)]
    s01 = part[0] + part[1]
    s0123 = s01 + (part[2] + part[3])
    s45 = part[4] + part[5]
    totals[z] = s0123 + (s45 + (part[6] + part[7]))

    def to_row(a, b):
        sem = tot_send.at[TARGETS[a].index(b) if a < b else 3]
        first_in = min([c for c, t in PAIRS if t == b] or [0])
        return remote(totals.at[a], totals.at[a], sem, tot_recv.at[a - first_in], device(b, y, core))

    for a in TO_FIRST:
        launch(to_row(a, 0), z == a)
    for a, b in FORWARD:

        @pl.when(z == a)
        def _():
            pl.semaphore_wait(ready.at[TARGETS[a].index(b)], 1)

        if (a, b) in PAIRS:
            launch(to_row(a, b), z == a)

    ring_sum[0] = s01.astype(BF16)
    ring_sum[1] = s45.astype(BF16)
    ring_sum[2] = s0123.astype(BF16)

    def low_copy(level, d):
        target = row_peer(d)
        src = ring_sum.at[target // 4] if level == 1 else ring_sum.at[2]
        return remote(
            src, low.at[level, y, mine, :], low_send.at[level - 1], low_recv.at[level - 1], device(z, target, core)
        )

    for d in FAR_FIRST:
        launch(low_copy(1, d), lax.rem(row_peer(d) // 2, 2) == 1, alone=False)
    for d in FAR_FIRST:
        launch(low_copy(2, d), jnp.logical_and(z == 0, row_peer(d) // 4 == 1), alone=False)
    for level in (1, 2):
        ends.append((y_bits[level], row_total(3, low_send.at[level - 1], ring_recv)))
        ends.append((jnp.logical_not(y_bits[level]), row_total(4, low_send.at[level - 1], ring_recv)))

    @pl.when(y_bits[1])
    def _():
        low[1, y, mine, :] = ring_sum[y // 4]

    @pl.when(y_bits[2])
    def _():
        low[2, y, mine, :] = ring_sum[2]

    for h in range(EARLY, HEADS_HERE):
        within(h)

    level_lanes = [slice(level * 128, (level + 1) * 128) for level in range(3)]
    for row in range(RING):
        rows_in = [a for a, b in PAIRS if b == row] if row else list(TO_FIRST)
        level = len(rows_in).bit_length() - 1 if row else 2

        @pl.when(z == row)
        def _():
            for a in rows_in:
                to_row(a, row).wait_recv()
            state = totals[rows_in[0]]
            for a in rows_in[1:] + [0] * (row == 0):
                state = state + totals[a]
            high[y, mine, level_lanes[level]] = state.astype(BF16)

    lowest = (1 - lax.rem(z, 2)) * (2 - lax.rem(z // 2, 2))
    lanes = pl.ds(pl.multiple_of(lowest * 128, 128), 128)

    def along_row(d):
        return remote(
            high.at[y, mine, lanes], high.at[y, mine, lanes], high_send, high_recv.at[d - 1],
            device(z, row_peer(d), core),
        )

    for d in FAR_FIRST:
        launch(along_row(d), alone=False)

    @pl.when(core == 1)
    def _():
        to_core1.wait_recv()
        for h in range(HEADS_HERE):
            acc[h] += w_cols[h, :, 2:3] * nn(q_s[h], core0[h])

    row_total(RING - 1, high_send, ring_recv).wait_send()
    for d in FAR_FIRST:
        launch(low_copy(2, d), jnp.logical_and(z > 0, row_peer(d) // 4 == 1), alone=False)

    def share_low(level):
        return remote(
            low.at[level, :, mine, :], low.at[level, :, mine, :], fwl_send.at[level], fwl_recv.at[level], sibling
        )

    arrivals = (0,) + NEAR_FIRST

    def share_high(i, h):
        return remote(high.at[h, mine, :], high.at[h, mine, :], fwh_send, fwh_recv.at[i], sibling)

    hop_to = jnp.where(z == 0, RING - 1, jnp.where(z == RING - 1, RING - 2, z + 1))

    def hop(level, i, h):
        ref = high.at[h, mine, level_lanes[level]]
        return remote(ref, ref, up_send.at[level - 1], up_recv.at[level - 1, i], device(hop_to, y, core))

    odd = z_bits[0]
    last = z == RING - 1
    hops = {1: lax.rem(z, 4) == 2, 2: jnp.logical_or(lax.rem(z, 4) == 0, last)}
    hop_in = {1: lax.rem(z, 4) == 3, 2: jnp.logical_or(z == 5, z == 6)}
    for i, d in enumerate(arrivals):
        h = lax.rem(y + RING - d, RING)
        if d:
            pl.when(jnp.logical_not(odd))(along_row(d).wait_recv)
        pl.when(last)(hop(2, i, h).wait_recv)
        for level in (2, 1):
            launch(hop(level, i, h), hops[level], alone=False)
    for level in (1, 2):
        ends.append((hops[level], row_total(RING, up_send.at[level - 1], ring_recv)))

    for level in range(3):

        @pl.when(y_bits[level])
        def _():
            if level == 0:
                to_next.wait_recv()
            else:
                row_total(RING - 1, ring_send, low_recv.at[level - 1]).wait_recv()

        launch(share_low(level), y_bits[level])

    for i, d in enumerate(arrivals):
        h = lax.rem(y + RING - d, RING)
        if d:
            pl.when(odd)(along_row(d).wait_recv)
        for level in (1, 2):
            pl.when(hop_in[level])(hop(level, i, h).wait_recv)
        launch(share_high(i, h), z > 0, alone=False)
    whole = high.at[:, mine, :]
    ends.append((z > 0, remote(whole, whole, fwh_send, fwh_recv.at[0], sibling)))

    for level in range(3):

        @pl.when(y_bits[level])
        def _():
            share_low(level).wait_recv()
            for h in range(HEADS_HERE):
                acc[h] += w_cols[h, :, 3 + level : 4 + level] * nn(q_s[h], low[level, h])

    @pl.when(z == 0)
    def _():
        total_sq = acc[0] * acc[0]
        for h in range(1, HEADS_HERE):
            total_sq += acc[h] * acc[h]
        sq[...] = total_sq

    @pl.when(z > 0)
    def _():
        for i, d in enumerate(arrivals):
            h = lax.rem(y + RING - d, RING)
            share_high(i, h).wait_recv()
            r = nn(q_s[h], high[h])
            a = acc[h]
            for level in range(3):
                a += w_cols[h, :, 6 + level : 7 + level] * r[:, level_lanes[level]]
            acc[h] = a
            if i == 0:
                sq[...] = a * a
            else:
                sq[...] += a * a

    sq_in[col, 0:1, :] = jnp.sum(sq[...].T, axis=0, keepdims=True)

    def to_cols(d):
        return remote(
            sq_in.at[col, 0:1], sq_in.at[col, 0:1], sq_send, sq_recv,
            (seq, lax.rem(col + d, COLS)),
        )

    for d in (2, 1, 3):
        launch(to_cols(d), alone=False)
    g_load.wait()
    others = sq_in.at[0 : COLS - 1, 0:1]
    from_cols = remote(others, others, sq_send, sq_recv, (seq, lax.rem(col + 1, COLS)))
    ends.append((None, from_cols))
    from_cols.wait_recv()
    squares = (sq_in[0, 0:1, :] + sq_in[1, 0:1, :]) + (sq_in[2, 0:1, :] + sq_in[3, 0:1, :])
    inverse = lax.rsqrt(squares / D + EPSILON)
    scale = jnp.broadcast_to(inverse, (HEAD_DIM, TOK)).T

    for h in range(HEADS_HERE):
        columns = slice(h * HEAD_DIM, (h + 1) * HEAD_DIM)
        out[:, columns] = (acc[h] * scale * g_v[:, columns]).astype(BF16)
    finish()


def local(queries, keys, values, level_weights, norm_gain):
    hd, tok, half, ring = HEAD_DIM, TOK, HALF, RING
    dma = pltpu.SemaphoreType.DMA
    any_space = pl.BlockSpec(memory_space=pl.ANY)
    scratch = [
        pltpu.VMEM((8, tok, hd), BF16),
        pltpu.VMEM((8, 2, tok, hd), BF16),
        pltpu.VMEM((9, 8, tok), F32),
        pltpu.VMEM((1, 1024), F32),
        pltpu.VMEM((8, 16, tok), F32),
        pltpu.VMEM((8, tok, 16), F32),
        pltpu.VMEM((8, hd, hd), BF16),
        pltpu.VMEM((8, hd, hd), F32),
        pltpu.VMEM((8, hd, hd), BF16),
        pltpu.VMEM((8, half, hd), F32),
        pltpu.VMEM((8, hd, hd), BF16),
        pltpu.VMEM((8, half, hd), BF16),
        pltpu.VMEM((ring, half, hd), BF16),
        pltpu.VMEM((3, half, hd), BF16),
        pltpu.VMEM((ring, half, hd), F32),
        pltpu.VMEM((3, 8, hd, hd), BF16),
        pltpu.VMEM((8, hd, 3 * hd), BF16),
        pltpu.VMEM((8, tok, hd), F32),
        pltpu.VMEM((tok, hd), F32),
        pltpu.VMEM((COLS, 8, tok), F32),
        dma((8,)), dma((3,)), pltpu.SemaphoreType.REGULAR((4,)),
        dma, dma((8,)), dma, dma, dma, dma, dma, dma,
        dma((2,)), dma((2,)), dma((4,)), dma((4,)), dma, dma((7,)), dma((2,)), dma((2, 8)),
        dma((3,)), dma((3,)), dma, dma((8,)), dma, dma,
    ]
    return pl.pallas_call(
        kernel,
        out_shape=pltpu.VMEM((tok, 8 * hd), BF16),
        in_specs=[any_space] * 5,
        out_specs=pl.BlockSpec(memory_space=pltpu.VMEM),
        scratch_shapes=scratch,
        compiler_params=pltpu.CompilerParams(
            collective_id=0, has_side_effects=True, vmem_limit_bytes=60 * 1024 * 1024
        ),
        cost_estimate=pl.CostEstimate(flops=2_000_000_000, bytes_accessed=4_400_000, transcendentals=0),
    )(queries, keys, values, level_weights, norm_gain.reshape(1, -1))


def solution(mesh):
    return jax.shard_map(
        local,
        mesh=mesh,
        in_specs=(
            P("seq", "head"),
            P("seq", "head"),
            P("seq", "head"),
            P(None, "head", "seq"),
            P("head"),
        ),
        out_specs=P("seq", "head"),
        check_vma=False,
    )
```

```python
import jax
import jax.numpy as jnp
from jax import lax
from jax.experimental import pallas as pl
from jax.experimental.pallas import tpu as pltpu
from jax.sharding import PartitionSpec as P

HEAD_DIM = 128
STRETCH = 256
D = 4096
EPSILON = 1e-06

RING = 8
COLS = 4
HEADS_HERE = 8
TOK = 512
LAG = 3
EARLY = 5
HALF = 64
FAR_FIRST = (4, 3, 5, 2, 6, 1, 7)
NEAR_FIRST = (1, 7, 2, 6, 3, 5, 4)
PAIRS = ((0, 1), (0, 2), (1, 2), (2, 3), (0, 4), (1, 4), (2, 4), (3, 4), (4, 5), (4, 6), (5, 6), (6, 7))
TO_FIRST = (1, 2, 3)
FORWARD = PAIRS + ((0, 6), (0, 7))
GREET = FORWARD + ((0, 3),)
TARGETS = {a: [b for c, b in FORWARD if c == a] for a in range(RING - 1)}
MESH = pl.DeviceIdType.MESH
F32 = jnp.float32
BF16 = jnp.bfloat16


def nt(a, b):
    return lax.dot_general(a, b, (((1,), (1,)), ((), ())), preferred_element_type=F32)


def tn(a, b):
    return lax.dot_general(a, b, (((0,), (0,)), ((), ())), preferred_element_type=F32)


def nn(a, b):
    return jnp.dot(a, b, preferred_element_type=F32)


def kernel(
    q_hbm, k_hbm, v_hbm, w_hbm, g_hbm, out,
    q_s, kv_s, w_v, g_v, w_rows, w_cols,
    first, own_sum, own_bf, pair_in, core0, chip_sum, ring_in, ring_sum, totals, low, high,
    acc, sq, sq_in,
    load_sem, misc_sem, ready,
    pair_send, pair_recv, core_send, core_recv, ring_send, ring_recv, next_send, next_recv,
    low_send, low_recv, tot_send, tot_recv, high_send, high_recv, up_send, up_recv,
    fwl_send, fwl_recv, fwh_send, fwh_recv, sq_send, sq_recv,
):
    seq = lax.axis_index("seq")
    col = lax.axis_index("head")
    core = lax.rem(seq, 2)
    y = lax.rem(seq // 2, RING)
    z = seq // (2 * RING)
    y_bits = (lax.rem(y, 2) == 1, lax.rem(y // 2, 2) == 1, y // 4 == 1)
    z_bits = (lax.rem(z, 2) == 1, lax.rem(z // 2, 2) == 1, z // 4 == 1)
    ends = []

    def device(z_, y_, core_):
        return (z_ * (2 * RING) + y_ * 2 + core_, col)

    sibling = device(z, y, 1 - core)
    mine = pl.ds(pl.multiple_of(core * HALF, HALF), HALF)
    other = pl.ds(pl.multiple_of((1 - core) * HALF, HALF), HALF)

    def row_peer(d):
        return lax.rem(y + d, RING)

    def remote(src, dst, send, recv, target):
        return pltpu.make_async_remote_copy(
            src_ref=src, dst_ref=dst, send_sem=send, recv_sem=recv, device_id=target, device_id_type=MESH
        )

    def when(cond, f):
        if cond is None:
            f()
        else:
            pl.when(cond)(f)

    def launch(copy, cond=None, alone=True):
        when(cond, copy.start)
        if alone:
            ends.append((cond, copy))

    def finish():
        for cond, copy in ends:
            when(cond, copy.wait_send)

    order = FAR_FIRST + (0,)

    def columns_of(i):
        return pl.ds(pl.multiple_of(row_peer(order[i]) * HEAD_DIM, HEAD_DIM), HEAD_DIM)

    for i, d in enumerate(order):
        pltpu.make_async_copy(k_hbm.at[:, columns_of(i)], kv_s.at[row_peer(d), 0], load_sem.at[i]).start()
        pltpu.make_async_copy(v_hbm.at[:, columns_of(i)], kv_s.at[row_peer(d), 1], load_sem.at[i]).start()
    w_load = pltpu.make_async_copy(w_hbm, w_v, misc_sem.at[0])
    g_load = pltpu.make_async_copy(g_hbm, g_v, misc_sem.at[1])

    barrier = pltpu.get_barrier_semaphore()

    def greet(target):
        pl.semaphore_signal(barrier, inc=1, device_id=target, device_id_type=MESH)

    for d in FAR_FIRST:
        greet(device(z, row_peer(d), core))
    for a, b in GREET:
        pl.when(z == a)(lambda: greet(device(b, y, core)))
    greet(sibling)
    for d in range(1, COLS):
        greet((seq, lax.rem(col + d, COLS)))

    for i, d in enumerate(order):
        pltpu.make_async_copy(q_hbm.at[:, columns_of(i)], q_s.at[row_peer(d)], misc_sem.at[2]).start()
    w_load.start()
    g_load.start()
    for level in range(3):

        @pl.when(jnp.logical_and(jnp.logical_not(z_bits[level]), z > 0))
        def _():
            high[:, mine, level * 128 : (level + 1) * 128] = jnp.zeros((HEADS_HERE, HALF, HEAD_DIM), BF16)

    @pl.when(jnp.logical_not(y_bits[2]))
    def _():
        high[:, :, 384:512] = jnp.zeros((HEADS_HERE, HEAD_DIM, HEAD_DIM), BF16)

    to_sibling = []
    for i, d in enumerate(order):
        h = row_peer(d)
        to_sibling.append(
            remote(own_sum.at[h, other, :], pair_in.at[h], pair_send, pair_recv.at[i], sibling)
        )
    for i, d in enumerate(order):
        h = row_peer(d)
        pltpu.make_async_copy(kv_s.at[h], kv_s.at[h], load_sem.at[i]).wait()
        k = kv_s[h, 0]
        v = kv_s[h, 1]
        s0 = tn(k[:STRETCH], v[:STRETCH])
        s1 = tn(k[STRETCH:], v[STRETCH:])
        first[h] = s0.astype(BF16)
        s = s0 + s1
        own_sum[h] = s
        own_bf[h] = s.astype(BF16)
        if i == 0:
            for row in range(RING):
                greeted = [a for a, b in GREET if b == row]

                @pl.when(z == row)
                def _():
                    pl.semaphore_wait(barrier, 1 + RING - 1 + COLS - 1 + len(greeted))
                    for a in [a for a, b in FORWARD if b == row]:
                        pl.semaphore_signal(
                            ready.at[TARGETS[a].index(row)], inc=1, device_id=device(a, y, core), device_id_type=MESH
                        )

        launch(to_sibling[i], alone=False)

    ends.append((None, remote(own_sum.at[:, other, :], pair_in, pair_send, pair_recv.at[0], sibling)))
    to_core1 = remote(own_bf, core0, core_send, core_recv, sibling)
    launch(to_core1, core == 0)

    def to_owner(d):
        h = row_peer(d)
        return remote(chip_sum.at[h], ring_in.at[y], ring_send, ring_recv, device(z, h, core))

    for i, d in enumerate(order):
        h = row_peer(d)
        to_sibling[i].wait_recv()
        c = (own_sum[h, mine, :] + pair_in[h]).astype(BF16)
        chip_sum[h] = c
        if d:
            launch(to_owner(d), alone=False)
        else:
            ring_in[y] = c

    def row_total(count, send, recv):
        return remote(chip_sum.at[0:count], ring_in.at[0:count], send, recv, device(z, row_peer(1), core))

    from_row = row_total(RING - 1, ring_send, ring_recv)
    ends.append((None, from_row))

    w_load.wait()
    for h in range(HEADS_HERE):
        for level in range(9):
            w_rows[h, level : level + 1, :] = w_v[level, h : h + 1, :]
        w_rows[h, 9:16, :] = jnp.zeros((7, TOK), F32)
    for h in range(HEADS_HERE):
        w_cols[h] = w_rows[h].T

    pltpu.make_async_copy(q_s, q_s, misc_sem.at[2]).wait()

    causal = lax.broadcasted_iota(jnp.int32, (STRETCH, STRETCH), 0) >= lax.broadcasted_iota(
        jnp.int32, (STRETCH, STRETCH), 1
    )

    def within(h):
        for s in range(2):
            rows = slice(s * STRETCH, (s + 1) * STRETCH)
            qs = q_s[h, rows, :]
            probs = jnp.where(causal, nt(qs, kv_s[h, 0, rows, :]), 0.0).astype(BF16)
            part = w_cols[h, rows, 0:1] * nn(probs, kv_s[h, 1, rows, :])
            if s == 1:
                part += w_cols[h, rows, 1:2] * nn(qs, first[h])
            acc[h, rows, :] = part

    for h in range(0, EARLY):
        within(h)

    to_next = remote(
        chip_sum, low.at[0, :, mine, :], next_send, next_recv, device(z, lax.rem(y + 1, RING), core)
    )
    launch(to_next, jnp.logical_not(y_bits[0]))

    from_row.wait_recv()
    part = [ring_in[j].astype(F32) for j in range(RING)]
    s01 = part[0] + part[1]
    s0123 = s01 + (part[2] + part[3])
    s45 = part[4] + part[5]
    totals[z] = s0123 + (s45 + (part[6] + part[7]))

    def to_row(a, b):
        sem = tot_send.at[TARGETS[a].index(b) if a < b else 3]
        first_in = min([c for c, t in PAIRS if t == b] or [0])
        return remote(totals.at[a], totals.at[a], sem, tot_recv.at[a - first_in], device(b, y, core))

    for a in TO_FIRST:
        launch(to_row(a, 0), z == a)
    for a, b in FORWARD:

        @pl.when(z == a)
        def _():
            pl.semaphore_wait(ready.at[TARGETS[a].index(b)], 1)

        if (a, b) in PAIRS:
            launch(to_row(a, b), z == a)

    ring_sum[0] = s01.astype(BF16)
    ring_sum[1] = s45.astype(BF16)
    ring_sum[2] = s0123.astype(BF16)

    def low_copy(level, d):
        target = row_peer(d)
        src = ring_sum.at[target // 4] if level == 1 else ring_sum.at[2]
        dst = low.at[1, y, mine, :] if level == 1 else high.at[y, mine, 384:512]
        return remote(
            src, dst, low_send.at[level - 1], low_recv.at[level - 1], device(z, target, core)
        )

    for d in FAR_FIRST:
        launch(low_copy(1, d), lax.rem(row_peer(d) // 2, 2) == 1, alone=False)
    for d in FAR_FIRST:
        launch(low_copy(2, d), jnp.logical_and(z == 0, row_peer(d) // 4 == 1), alone=False)
    for level in (1, 2):
        ends.append((y_bits[level], row_total(3, low_send.at[level - 1], ring_recv)))
        ends.append((jnp.logical_not(y_bits[level]), row_total(4, low_send.at[level - 1], ring_recv)))

    @pl.when(y_bits[1])
    def _():
        low[1, y, mine, :] = ring_sum[y // 4]

    @pl.when(y_bits[2])
    def _():
        high[y, mine, 384:512] = ring_sum[2]

    for h in range(EARLY, HEADS_HERE):
        within(h)

    level_lanes = [slice(level * 128, (level + 1) * 128) for level in range(3)]
    for row in range(RING):
        rows_in = [a for a, b in PAIRS if b == row] if row else list(TO_FIRST)
        level = len(rows_in).bit_length() - 1 if row else 2

        @pl.when(z == row)
        def _():
            for a in rows_in:
                to_row(a, row).wait_recv()
            state = totals[rows_in[0]]
            for a in rows_in[1:] + [0] * (row == 0):
                state = state + totals[a]
            high[y, mine, level_lanes[level]] = state.astype(BF16)

    lowest = (1 - lax.rem(z, 2)) * (2 - lax.rem(z // 2, 2))
    lanes = pl.ds(pl.multiple_of(lowest * 128, 128), 128)

    def along_row(d):
        return remote(
            high.at[y, mine, lanes], high.at[y, mine, lanes], high_send, high_recv.at[d - 1],
            device(z, row_peer(d), core),
        )

    for d in NEAR_FIRST:
        launch(along_row(d), alone=False)

    @pl.when(core == 1)
    def _():
        to_core1.wait_recv()
        for h in range(HEADS_HERE):
            acc[h] += w_cols[h, :, 2:3] * nn(q_s[h], core0[h])

    row_total(RING - 1, high_send, ring_recv).wait_send()
    for d in FAR_FIRST:
        launch(low_copy(2, d), jnp.logical_and(z > 0, row_peer(d) // 4 == 1), alone=False)

    def share_low(level):
        part = low.at[level, :, mine, :] if level < 2 else high.at[:, mine, 384:512]
        return remote(part, part, fwl_send.at[level], fwl_recv.at[level], sibling)

    def low_arrival(level, cond):
        @pl.when(cond)
        def _():
            if level == 0:
                to_next.wait_recv()
            else:
                row_total(RING - 1, ring_send, low_recv.at[level - 1]).wait_recv()
            share_low(level).start()

    for level in range(3):
        ends.append((y_bits[level], share_low(level)))
    low_arrival(0, y_bits[0])
    low_arrival(1, y_bits[1])
    low_arrival(2, jnp.logical_and(y_bits[2], z == 0))

    def low_readout(level):
        @pl.when(y_bits[level])
        def _():
            share_low(level).wait_recv()
            for h in range(HEADS_HERE):
                acc[h] += w_cols[h, :, 3 + level : 4 + level] * nn(q_s[h], low[level, h])

    arrivals = (0,) + NEAR_FIRST

    def share_high(i, h):
        part = high.at[h, mine, 0:384]
        return remote(part, part, fwh_send, fwh_recv.at[i], sibling)

    def hop(level, i, h, to):
        ref = high.at[h, mine, level_lanes[level]]
        return remote(ref, ref, up_send.at[level - 1], up_recv.at[level - 1, i], device(to, y, core))

    odd = z_bits[0]
    above = lax.rem(z + 1, RING)
    hop_in = {1: lax.rem(z, 4) == 3, 2: z > 4}
    @pl.when(z == 0)
    def _():
        low_readout(0)
        low_readout(1)
        pl.when(y_bits[2])(share_low(2).wait_recv)
        for h in range(HEADS_HERE):
            a = acc[h] + w_cols[h, :, 5:6] * nn(q_s[h], high[h, :, 384:512])
            acc[h] = a
            sq[...] = a * a if h == 0 else sq[...] + a * a

    for i, d in enumerate(arrivals):
        h = lax.rem(y + RING - d, RING)
        if d:
            pl.when(jnp.logical_not(odd))(along_row(d).wait_recv)
        for to in (RING - 2, RING - 1):
            launch(hop(2, i, h, to), z == 0, alone=False)
        launch(hop(2, i, h, above), z == 4, alone=False)
        launch(hop(1, i, h, above), lax.rem(z, 4) == 2, alone=False)
    ends.append((lax.rem(z, 4) == 2, row_total(RING, up_send.at[0], ring_recv)))
    ends.append((z == 4, row_total(RING, up_send.at[1], ring_recv)))
    ends.append((z == 0, remote(low.at[0], low.at[0], up_send.at[1], ring_recv, sibling)))

    def readout(i, d):
        h = lax.rem(y + RING - d, RING)
        share_high(i, h).wait_recv()
        r = nn(q_s[h], high[h])
        a = acc[h] + w_cols[h, :, 5:6] * r[:, 384:512]
        for level in range(3):
            a += w_cols[h, :, 6 + level : 7 + level] * r[:, level_lanes[level]]
        acc[h] = a
        sq[...] = a * a if i == 0 else sq[...] + a * a

    @pl.when(z > 0)
    def _():
        low_readout(0)
        low_readout(1)
        low_arrival(2, y_bits[2])
        for i, d in enumerate(arrivals):
            h = lax.rem(y + RING - d, RING)
            if d:
                pl.when(odd)(along_row(d).wait_recv)
            for level in (1, 2):
                pl.when(hop_in[level])(hop(level, i, h, above).wait_recv)
            share_high(i, h).start()
            if i == LAG:
                pl.when(y_bits[2])(share_low(2).wait_recv)
            if i >= LAG:
                readout(i - LAG, arrivals[i - LAG])
        for i in range(RING - LAG, RING):
            readout(i, arrivals[i])

    whole = high.at[:, mine, 0:384]
    ends.append((z > 0, remote(whole, whole, fwh_send, fwh_recv.at[0], sibling)))

    sq_in[col, 0:1, :] = jnp.sum(sq[...].T, axis=0, keepdims=True)

    def to_cols(d):
        return remote(
            sq_in.at[col, 0:1], sq_in.at[col, 0:1], sq_send, sq_recv,
            (seq, lax.rem(col + d, COLS)),
        )

    for d in (2, 1, 3):
        launch(to_cols(d), alone=False)
    g_load.wait()
    others = sq_in.at[0 : COLS - 1, 0:1]
    from_cols = remote(others, others, sq_send, sq_recv, (seq, lax.rem(col + 1, COLS)))
    ends.append((None, from_cols))
    from_cols.wait_recv()
    squares = (sq_in[0, 0:1, :] + sq_in[1, 0:1, :]) + (sq_in[2, 0:1, :] + sq_in[3, 0:1, :])
    inverse = lax.rsqrt(squares / D + EPSILON)
    scale = jnp.broadcast_to(inverse, (HEAD_DIM, TOK)).T

    for h in range(HEADS_HERE):
        columns = slice(h * HEAD_DIM, (h + 1) * HEAD_DIM)
        out[:, columns] = (acc[h] * scale * g_v[:, columns]).astype(BF16)
    finish()


def local(queries, keys, values, level_weights, norm_gain):
    hd, tok, half, ring = HEAD_DIM, TOK, HALF, RING
    dma = pltpu.SemaphoreType.DMA
    any_space = pl.BlockSpec(memory_space=pl.ANY)
    scratch = [
        pltpu.VMEM((8, tok, hd), BF16),
        pltpu.VMEM((8, 2, tok, hd), BF16),
        pltpu.VMEM((9, 8, tok), F32),
        pltpu.VMEM((1, 1024), F32),
        pltpu.VMEM((8, 16, tok), F32),
        pltpu.VMEM((8, tok, 16), F32),
        pltpu.VMEM((8, hd, hd), BF16),
        pltpu.VMEM((8, hd, hd), F32),
        pltpu.VMEM((8, hd, hd), BF16),
        pltpu.VMEM((8, half, hd), F32),
        pltpu.VMEM((8, hd, hd), BF16),
        pltpu.VMEM((8, half, hd), BF16),
        pltpu.VMEM((ring, half, hd), BF16),
        pltpu.VMEM((3, half, hd), BF16),
        pltpu.VMEM((ring, half, hd), F32),
        pltpu.VMEM((2, 8, hd, hd), BF16),
        pltpu.VMEM((8, hd, 4 * hd), BF16),
        pltpu.VMEM((8, tok, hd), F32),
        pltpu.VMEM((tok, hd), F32),
        pltpu.VMEM((COLS, 8, tok), F32),
        dma((8,)), dma((3,)), pltpu.SemaphoreType.REGULAR((5,)),
        dma, dma((8,)), dma, dma, dma, dma, dma, dma,
        dma((2,)), dma((2,)), dma((4,)), dma((4,)), dma, dma((7,)), dma((2,)), dma((2, 8)),
        dma((3,)), dma((3,)), dma, dma((8,)), dma, dma,
    ]
    return pl.pallas_call(
        kernel,
        out_shape=pltpu.VMEM((tok, 8 * hd), BF16),
        in_specs=[any_space] * 5,
        out_specs=pl.BlockSpec(memory_space=pltpu.VMEM),
        scratch_shapes=scratch,
        compiler_params=pltpu.CompilerParams(
            collective_id=0, has_side_effects=True, vmem_limit_bytes=60 * 1024 * 1024
        ),
        cost_estimate=pl.CostEstimate(flops=2_000_000_000, bytes_accessed=4_400_000, transcendentals=0),
    )(queries, keys, values, level_weights, norm_gain.reshape(1, -1))


def solution(mesh):
    return jax.shard_map(
        local,
        mesh=mesh,
        in_specs=(
            P("seq", "head"),
            P("seq", "head"),
            P("seq", "head"),
            P(None, "head", "seq"),
            P("head"),
        ),
        out_specs=P("seq", "head"),
        check_vma=False,
    )
```

```python
import jax
import jax.numpy as jnp
from jax import lax
from jax.experimental import pallas as pl
from jax.experimental.pallas import tpu as pltpu
from jax.sharding import PartitionSpec as P

HEAD_DIM = 128
STRETCH = 256
D = 4096
EPSILON = 1e-06

RING = 8
COLS = 4
HEADS_HERE = 8
TOK = 512
LAG = 3
EARLY = 3
HALF = 64
FAR_FIRST = (4, 3, 5, 2, 6, 1, 7)
NEAR_FIRST = (1, 7, 2, 6, 3, 5, 4)
PAIRS = ((0, 1), (0, 2), (1, 2), (2, 3), (0, 4), (1, 4), (2, 4), (3, 4), (4, 5), (4, 6), (5, 6), (6, 7))
TO_FIRST = (1, 2, 3)
FORWARD = PAIRS + ((0, 6), (0, 7))
GREET = FORWARD + ((0, 3),)
TARGETS = {a: [b for c, b in FORWARD if c == a] for a in range(RING - 1)}
MESH = pl.DeviceIdType.MESH
F32 = jnp.float32
BF16 = jnp.bfloat16


def nt(a, b):
    return lax.dot_general(a, b, (((1,), (1,)), ((), ())), preferred_element_type=F32)


def tn(a, b):
    return lax.dot_general(a, b, (((0,), (0,)), ((), ())), preferred_element_type=F32)


def nn(a, b):
    return jnp.dot(a, b, preferred_element_type=F32)


def kernel(
    q_hbm, k_hbm, v_hbm, w_hbm, g_hbm, out,
    q_s, kv_s, w_v, g_v, w_rows, w_cols,
    first, own_sum, own_bf, pair_in, core0, chip_sum, ring_in, ring_sum, totals, low, high,
    acc, sq, sq_in,
    load_sem, misc_sem, ready,
    pair_send, pair_recv, core_send, core_recv, ring_send, ring_recv, next_send, next_recv,
    low_send, low_recv, tot_send, tot_recv, high_send, high_recv, up_send, up_recv,
    fwl_send, fwl_recv, fwh_send, fwh_recv, sq_send, sq_recv,
):
    seq = lax.axis_index("seq")
    col = lax.axis_index("head")
    core = lax.rem(seq, 2)
    y = lax.rem(seq // 2, RING)
    z = seq // (2 * RING)
    y_bits = (lax.rem(y, 2) == 1, lax.rem(y // 2, 2) == 1, y // 4 == 1)
    z_bits = (lax.rem(z, 2) == 1, lax.rem(z // 2, 2) == 1, z // 4 == 1)
    ends = []

    def device(z_, y_, core_):
        return (z_ * (2 * RING) + y_ * 2 + core_, col)

    sibling = device(z, y, 1 - core)
    mine = pl.ds(pl.multiple_of(core * HALF, HALF), HALF)
    other = pl.ds(pl.multiple_of((1 - core) * HALF, HALF), HALF)

    def row_peer(d):
        return lax.rem(y + d, RING)

    def remote(src, dst, send, recv, target):
        return pltpu.make_async_remote_copy(
            src_ref=src, dst_ref=dst, send_sem=send, recv_sem=recv, device_id=target, device_id_type=MESH
        )

    def when(cond, f):
        if cond is None:
            f()
        else:
            pl.when(cond)(f)

    def launch(copy, cond=None, alone=True):
        when(cond, copy.start)
        if alone:
            ends.append((cond, copy))

    def finish():
        for cond, copy in ends:
            when(cond, copy.wait_send)

    order = FAR_FIRST + (0,)

    def columns_of(i):
        return pl.ds(pl.multiple_of(row_peer(order[i]) * HEAD_DIM, HEAD_DIM), HEAD_DIM)

    for i, d in enumerate(order):
        pltpu.make_async_copy(k_hbm.at[:, columns_of(i)], kv_s.at[row_peer(d), 0], load_sem.at[i]).start()
        pltpu.make_async_copy(v_hbm.at[:, columns_of(i)], kv_s.at[row_peer(d), 1], load_sem.at[i]).start()
    w_load = pltpu.make_async_copy(w_hbm, w_v, misc_sem.at[0])
    g_load = pltpu.make_async_copy(g_hbm, g_v, misc_sem.at[1])

    barrier = pltpu.get_barrier_semaphore()

    def greet(target):
        pl.semaphore_signal(barrier, inc=1, device_id=target, device_id_type=MESH)

    for d in FAR_FIRST:
        greet(device(z, row_peer(d), core))
    for a, b in GREET:
        pl.when(z == a)(lambda: greet(device(b, y, core)))
    greet(sibling)
    for d in range(1, COLS):
        greet((seq, lax.rem(col + d, COLS)))

    for i, d in enumerate(order):
        pltpu.make_async_copy(q_hbm.at[:, columns_of(i)], q_s.at[row_peer(d)], misc_sem.at[2]).start()
    w_load.start()
    g_load.start()
    for level in range(3):

        @pl.when(jnp.logical_and(jnp.logical_not(z_bits[level]), z > 0))
        def _():
            high[:, mine, level * 128 : (level + 1) * 128] = jnp.zeros((HEADS_HERE, HALF, HEAD_DIM), BF16)

    @pl.when(jnp.logical_not(y_bits[2]))
    def _():
        high[:, :, 384:512] = jnp.zeros((HEADS_HERE, HEAD_DIM, HEAD_DIM), BF16)

    to_sibling = []
    for i, d in enumerate(order):
        h = row_peer(d)
        to_sibling.append(
            remote(own_sum.at[h, other, :], pair_in.at[h], pair_send, pair_recv.at[i], sibling)
        )
    for i, d in enumerate(order):
        h = row_peer(d)
        pltpu.make_async_copy(kv_s.at[h], kv_s.at[h], load_sem.at[i]).wait()
        k = kv_s[h, 0]
        v = kv_s[h, 1]
        s0 = tn(k[:STRETCH], v[:STRETCH])
        s1 = tn(k[STRETCH:], v[STRETCH:])
        first[h] = s0.astype(BF16)
        s = s0 + s1
        own_sum[h] = s
        own_bf[h] = s.astype(BF16)
        if i == 0:
            for row in range(RING):
                greeted = [a for a, b in GREET if b == row]

                @pl.when(z == row)
                def _():
                    pl.semaphore_wait(barrier, 1 + RING - 1 + COLS - 1 + len(greeted))
                    for a in [a for a, b in FORWARD if b == row]:
                        pl.semaphore_signal(
                            ready.at[TARGETS[a].index(row)], inc=1, device_id=device(a, y, core), device_id_type=MESH
                        )

        launch(to_sibling[i], alone=False)

    ends.append((None, remote(own_sum.at[:, other, :], pair_in, pair_send, pair_recv.at[0], sibling)))
    to_core1 = remote(own_bf, core0, core_send, core_recv, sibling)
    launch(to_core1, core == 0)

    def to_owner(d):
        h = row_peer(d)
        return remote(chip_sum.at[h], ring_in.at[y], ring_send, ring_recv, device(z, h, core))

    for i, d in enumerate(order):
        h = row_peer(d)
        to_sibling[i].wait_recv()
        c = (own_sum[h, mine, :] + pair_in[h]).astype(BF16)
        chip_sum[h] = c
        if d:
            launch(to_owner(d), alone=False)
        else:
            ring_in[y] = c

    def row_total(count, send, recv):
        return remote(chip_sum.at[0:count], ring_in.at[0:count], send, recv, device(z, row_peer(1), core))

    from_row = row_total(RING - 1, ring_send, ring_recv)
    ends.append((None, from_row))

    w_load.wait()
    for h in range(HEADS_HERE):
        for level in range(9):
            w_rows[h, level : level + 1, :] = w_v[level, h : h + 1, :]
        w_rows[h, 9:16, :] = jnp.zeros((7, TOK), F32)
    for h in range(HEADS_HERE):
        w_cols[h] = w_rows[h].T

    pltpu.make_async_copy(q_s, q_s, misc_sem.at[2]).wait()

    causal = lax.broadcasted_iota(jnp.int32, (STRETCH, STRETCH), 0) >= lax.broadcasted_iota(
        jnp.int32, (STRETCH, STRETCH), 1
    )

    def within(h):
        for s in range(2):
            rows = slice(s * STRETCH, (s + 1) * STRETCH)
            qs = q_s[h, rows, :]
            probs = jnp.where(causal, nt(qs, kv_s[h, 0, rows, :]), 0.0).astype(BF16)
            part = w_cols[h, rows, 0:1] * nn(probs, kv_s[h, 1, rows, :])
            if s == 1:
                part += w_cols[h, rows, 1:2] * nn(qs, first[h])
            acc[h, rows, :] = part

    for h in range(0, EARLY):
        within(h)

    to_next = remote(
        chip_sum, low.at[0, :, mine, :], next_send, next_recv, device(z, lax.rem(y + 1, RING), core)
    )
    launch(to_next, jnp.logical_not(y_bits[0]))

    from_row.wait_recv()
    part = [ring_in[j].astype(F32) for j in range(RING)]
    s01 = part[0] + part[1]
    s0123 = s01 + (part[2] + part[3])
    s45 = part[4] + part[5]
    totals[z] = s0123 + (s45 + (part[6] + part[7]))

    def to_row(a, b):
        sem = tot_send.at[TARGETS[a].index(b) if a < b else 3]
        first_in = min([c for c, t in PAIRS if t == b] or [0])
        return remote(totals.at[a], totals.at[a], sem, tot_recv.at[a - first_in], device(b, y, core))

    for a in TO_FIRST:
        launch(to_row(a, 0), z == a)
    for a, b in FORWARD:

        @pl.when(z == a)
        def _():
            pl.semaphore_wait(ready.at[TARGETS[a].index(b)], 1)

        if (a, b) in PAIRS:
            launch(to_row(a, b), z == a)

    ring_sum[0] = s01.astype(BF16)
    ring_sum[1] = s45.astype(BF16)
    ring_sum[2] = s0123.astype(BF16)

    def low_copy(level, d):
        target = row_peer(d)
        src = ring_sum.at[target // 4] if level == 1 else ring_sum.at[2]
        dst = low.at[1, y, mine, :] if level == 1 else high.at[y, mine, 384:512]
        return remote(
            src, dst, low_send.at[level - 1], low_recv.at[level - 1], device(z, target, core)
        )

    for d in FAR_FIRST:
        launch(low_copy(1, d), lax.rem(row_peer(d) // 2, 2) == 1, alone=False)
    for d in FAR_FIRST:
        launch(low_copy(2, d), jnp.logical_and(z == 0, row_peer(d) // 4 == 1), alone=False)
    for level in (1, 2):
        ends.append((y_bits[level], row_total(3, low_send.at[level - 1], ring_recv)))
        ends.append((jnp.logical_not(y_bits[level]), row_total(4, low_send.at[level - 1], ring_recv)))

    @pl.when(y_bits[1])
    def _():
        low[1, y, mine, :] = ring_sum[y // 4]

    @pl.when(y_bits[2])
    def _():
        high[y, mine, 384:512] = ring_sum[2]

    for h in range(EARLY, HEADS_HERE):
        within(h)

    level_lanes = [slice(level * 128, (level + 1) * 128) for level in range(3)]
    for row in range(RING):
        rows_in = [a for a, b in PAIRS if b == row] if row else list(TO_FIRST)
        level = len(rows_in).bit_length() - 1 if row else 2

        @pl.when(z == row)
        def _():
            for a in rows_in:
                to_row(a, row).wait_recv()
            state = totals[rows_in[0]]
            for a in rows_in[1:] + [0] * (row == 0):
                state = state + totals[a]
            high[y, mine, level_lanes[level]] = state.astype(BF16)

    lowest = (1 - lax.rem(z, 2)) * (2 - lax.rem(z // 2, 2))
    lanes = pl.ds(pl.multiple_of(lowest * 128, 128), 128)

    def along_row(d):
        return remote(
            high.at[y, mine, lanes], high.at[y, mine, lanes], high_send, high_recv.at[d - 1],
            device(z, row_peer(d), core),
        )

    for d in NEAR_FIRST:
        launch(along_row(d), alone=False)

    @pl.when(core == 1)
    def _():
        to_core1.wait_recv()
        for h in range(HEADS_HERE):
            acc[h] += w_cols[h, :, 2:3] * nn(q_s[h], core0[h])

    row_total(RING - 1, high_send, ring_recv).wait_send()
    for d in FAR_FIRST:
        launch(low_copy(2, d), jnp.logical_and(z > 0, row_peer(d) // 4 == 1), alone=False)

    def share_low(level):
        part = low.at[level, :, mine, :] if level < 2 else high.at[:, mine, 384:512]
        return remote(part, part, fwl_send.at[level], fwl_recv.at[level], sibling)

    def low_arrival(level, cond):
        @pl.when(cond)
        def _():
            if level == 0:
                to_next.wait_recv()
            else:
                row_total(RING - 1, ring_send, low_recv.at[level - 1]).wait_recv()
            share_low(level).start()

    for level in range(3):
        ends.append((y_bits[level], share_low(level)))
    low_arrival(0, y_bits[0])
    low_arrival(1, y_bits[1])
    low_arrival(2, jnp.logical_and(y_bits[2], z == 0))

    def low_readout(level):
        @pl.when(y_bits[level])
        def _():
            share_low(level).wait_recv()
            for h in range(HEADS_HERE):
                acc[h] += w_cols[h, :, 3 + level : 4 + level] * nn(q_s[h], low[level, h])

    arrivals = (0,) + NEAR_FIRST

    def share_high(i, h):
        part = high.at[h, mine, 0:384]
        return remote(part, part, fwh_send, fwh_recv.at[i], sibling)

    def hop(level, i, h, to):
        ref = high.at[h, mine, level_lanes[level]]
        return remote(ref, ref, up_send.at[level - 1], up_recv.at[level - 1, i], device(to, y, core))

    odd = z_bits[0]
    above = lax.rem(z + 1, RING)
    hop_in = {1: lax.rem(z, 4) == 3, 2: z > 4}
    @pl.when(z == 0)
    def _():
        low_readout(0)
        low_readout(1)
        pl.when(y_bits[2])(share_low(2).wait_recv)
        for h in range(HEADS_HERE):
            a = acc[h] + w_cols[h, :, 5:6] * nn(q_s[h], high[h, :, 384:512])
            acc[h] = a
            sq[...] = a * a if h == 0 else sq[...] + a * a

    for i, d in enumerate(arrivals):
        h = lax.rem(y + RING - d, RING)
        if d:
            pl.when(jnp.logical_not(odd))(along_row(d).wait_recv)
        for to in (RING - 2, RING - 1):
            launch(hop(2, i, h, to), z == 0, alone=False)
        launch(hop(2, i, h, above), z == 4, alone=False)
        launch(hop(1, i, h, above), lax.rem(z, 4) == 2, alone=False)
    ends.append((lax.rem(z, 4) == 2, row_total(RING, up_send.at[0], ring_recv)))
    ends.append((z == 4, row_total(RING, up_send.at[1], ring_recv)))
    ends.append((z == 0, remote(low.at[0], low.at[0], up_send.at[1], ring_recv, sibling)))

    def readout(i, d):
        h = lax.rem(y + RING - d, RING)
        share_high(i, h).wait_recv()
        r = nn(q_s[h], high[h])
        a = acc[h] + w_cols[h, :, 5:6] * r[:, 384:512]
        for level in range(3):
            a += w_cols[h, :, 6 + level : 7 + level] * r[:, level_lanes[level]]
        acc[h] = a
        sq[...] = a * a if i == 0 else sq[...] + a * a

    @pl.when(z > 0)
    def _():
        low_readout(0)
        low_readout(1)
        low_arrival(2, y_bits[2])
        for i, d in enumerate(arrivals):
            h = lax.rem(y + RING - d, RING)
            if d:
                pl.when(odd)(along_row(d).wait_recv)
            for level in (1, 2):
                pl.when(hop_in[level])(hop(level, i, h, above).wait_recv)
            share_high(i, h).start()
            if i == LAG:
                pl.when(y_bits[2])(share_low(2).wait_recv)
            if i >= LAG:
                readout(i - LAG, arrivals[i - LAG])
        for i in range(RING - LAG, RING):
            readout(i, arrivals[i])

    whole = high.at[:, mine, 0:384]
    ends.append((z > 0, remote(whole, whole, fwh_send, fwh_recv.at[0], sibling)))

    sq_in[col, 0:1, :] = jnp.sum(sq[...].T, axis=0, keepdims=True)

    def to_cols(d):
        return remote(
            sq_in.at[col, 0:1], sq_in.at[col, 0:1], sq_send, sq_recv,
            (seq, lax.rem(col + d, COLS)),
        )

    for d in (2, 1, 3):
        launch(to_cols(d), alone=False)
    g_load.wait()
    for h in range(HEADS_HERE):
        acc[h] = acc[h] * g_v[:, h * HEAD_DIM : (h + 1) * HEAD_DIM]
    others = sq_in.at[0 : COLS - 1, 0:1]
    from_cols = remote(others, others, sq_send, sq_recv, (seq, lax.rem(col + 1, COLS)))
    ends.append((None, from_cols))
    from_cols.wait_recv()
    squares = (sq_in[0, 0:1, :] + sq_in[1, 0:1, :]) + (sq_in[2, 0:1, :] + sq_in[3, 0:1, :])
    inverse = lax.rsqrt(squares / D + EPSILON)
    scale = jnp.broadcast_to(inverse, (HEAD_DIM, TOK)).T

    for h in range(HEADS_HERE):
        columns = slice(h * HEAD_DIM, (h + 1) * HEAD_DIM)
        out[:, columns] = (acc[h] * scale).astype(BF16)
    finish()


def local(queries, keys, values, level_weights, norm_gain):
    hd, tok, half, ring = HEAD_DIM, TOK, HALF, RING
    dma = pltpu.SemaphoreType.DMA
    any_space = pl.BlockSpec(memory_space=pl.ANY)
    scratch = [
        pltpu.VMEM((8, tok, hd), BF16),
        pltpu.VMEM((8, 2, tok, hd), BF16),
        pltpu.VMEM((9, 8, tok), F32),
        pltpu.VMEM((1, 1024), F32),
        pltpu.VMEM((8, 16, tok), F32),
        pltpu.VMEM((8, tok, 16), F32),
        pltpu.VMEM((8, hd, hd), BF16),
        pltpu.VMEM((8, hd, hd), F32),
        pltpu.VMEM((8, hd, hd), BF16),
        pltpu.VMEM((8, half, hd), F32),
        pltpu.VMEM((8, hd, hd), BF16),
        pltpu.VMEM((8, half, hd), BF16),
        pltpu.VMEM((ring, half, hd), BF16),
        pltpu.VMEM((3, half, hd), BF16),
        pltpu.VMEM((ring, half, hd), F32),
        pltpu.VMEM((2, 8, hd, hd), BF16),
        pltpu.VMEM((8, hd, 4 * hd), BF16),
        pltpu.VMEM((8, tok, hd), F32),
        pltpu.VMEM((tok, hd), F32),
        pltpu.VMEM((COLS, 8, tok), F32),
        dma((8,)), dma((3,)), pltpu.SemaphoreType.REGULAR((5,)),
        dma, dma((8,)), dma, dma, dma, dma, dma, dma,
        dma((2,)), dma((2,)), dma((4,)), dma((4,)), dma, dma((7,)), dma((2,)), dma((2, 8)),
        dma((3,)), dma((3,)), dma, dma((8,)), dma, dma,
    ]
    return pl.pallas_call(
        kernel,
        out_shape=pltpu.VMEM((tok, 8 * hd), BF16),
        in_specs=[any_space] * 5,
        out_specs=pl.BlockSpec(memory_space=pltpu.VMEM),
        scratch_shapes=scratch,
        compiler_params=pltpu.CompilerParams(
            collective_id=0, has_side_effects=True, vmem_limit_bytes=60 * 1024 * 1024
        ),
        cost_estimate=pl.CostEstimate(flops=2_000_000_000, bytes_accessed=4_400_000, transcendentals=0),
    )(queries, keys, values, level_weights, norm_gain.reshape(1, -1))


def solution(mesh):
    return jax.shard_map(
        local,
        mesh=mesh,
        in_specs=(
            P("seq", "head"),
            P("seq", "head"),
            P("seq", "head"),
            P(None, "head", "seq"),
            P("head"),
        ),
        out_specs=P("seq", "head"),
        check_vma=False,
    )
```

```python
import jax
import jax.numpy as jnp
from jax import lax
from jax.experimental import pallas as pl
from jax.experimental.pallas import tpu as pltpu
from jax.sharding import PartitionSpec as P

HEAD_DIM = 128
STRETCH = 256
D = 4096
EPSILON = 1e-06

RING = 8
COLS = 4
HEADS_HERE = 8
TOK = 512
LAG = 3
EARLY = 3
HALF = 64
FAR_FIRST = (4, 3, 5, 2, 6, 1, 7)
NEAR_FIRST = (1, 7, 2, 6, 3, 5, 4)
PAIRS = ((0, 1), (0, 2), (1, 2), (2, 3), (0, 4), (1, 4), (2, 4), (3, 4), (4, 5), (4, 6), (5, 6), (6, 7))
TO_FIRST = (1, 2, 3)
FORWARD = PAIRS + ((0, 6), (0, 7))
GREET = FORWARD + ((0, 3),)
TARGETS = {a: [b for c, b in FORWARD if c == a] for a in range(RING - 1)}
MESH = pl.DeviceIdType.MESH
F32 = jnp.float32
BF16 = jnp.bfloat16


def nt(a, b):
    return lax.dot_general(a, b, (((1,), (1,)), ((), ())), preferred_element_type=F32)


def tn(a, b):
    return lax.dot_general(a, b, (((0,), (0,)), ((), ())), preferred_element_type=F32)


def nn(a, b):
    return jnp.dot(a, b, preferred_element_type=F32)


def kernel(
    q_hbm, k_hbm, v_hbm, w_hbm, g_hbm, out,
    q_s, kv_s, w_v, g_v, w_rows, w_cols,
    first, own_sum, own_bf, pair_in, core0, chip_sum, ring_in, ring_sum, totals, low, high,
    acc, sq, sq_in,
    load_sem, misc_sem, ready,
    pair_send, pair_recv, core_send, core_recv, ring_send, ring_recv, next_send, next_recv,
    low_send, low_recv, tot_send, tot_recv, high_send, high_recv, up_send, up_recv,
    fwl_send, fwl_recv, fwh_send, fwh_recv, sq_send, sq_recv,
):
    seq = lax.axis_index("seq")
    col = lax.axis_index("head")
    core = lax.rem(seq, 2)
    y = lax.rem(seq // 2, RING)
    z = seq // (2 * RING)
    y_bits = (lax.rem(y, 2) == 1, lax.rem(y // 2, 2) == 1, y // 4 == 1)
    z_bits = (lax.rem(z, 2) == 1, lax.rem(z // 2, 2) == 1, z // 4 == 1)
    ends = []

    def device(z_, y_, core_):
        return (z_ * (2 * RING) + y_ * 2 + core_, col)

    sibling = device(z, y, 1 - core)
    mine = pl.ds(pl.multiple_of(core * HALF, HALF), HALF)
    other = pl.ds(pl.multiple_of((1 - core) * HALF, HALF), HALF)

    def row_peer(d):
        return lax.rem(y + d, RING)

    def remote(src, dst, send, recv, target):
        return pltpu.make_async_remote_copy(
            src_ref=src, dst_ref=dst, send_sem=send, recv_sem=recv, device_id=target, device_id_type=MESH
        )

    def when(cond, f):
        if cond is None:
            f()
        else:
            pl.when(cond)(f)

    def launch(copy, cond=None, alone=True):
        when(cond, copy.start)
        if alone:
            ends.append((cond, copy))

    def finish():
        for cond, copy in ends:
            when(cond, copy.wait_send)

    order = FAR_FIRST + (0,)

    def columns_of(i):
        return pl.ds(pl.multiple_of(row_peer(order[i]) * HEAD_DIM, HEAD_DIM), HEAD_DIM)

    def load_kv(i):
        h = row_peer(order[i])
        pltpu.make_async_copy(k_hbm.at[:, columns_of(i)], kv_s.at[h, 0], load_sem.at[i]).start()
        pltpu.make_async_copy(v_hbm.at[:, columns_of(i)], kv_s.at[h, 1], load_sem.at[i]).start()

    for i in range(2):
        load_kv(i)
    w_load = pltpu.make_async_copy(w_hbm, w_v, misc_sem.at[0])
    g_load = pltpu.make_async_copy(g_hbm, g_v, misc_sem.at[1])

    barrier = pltpu.get_barrier_semaphore()

    def greet(target):
        pl.semaphore_signal(barrier, inc=1, device_id=target, device_id_type=MESH)

    for d in FAR_FIRST:
        greet(device(z, row_peer(d), core))
    for i in range(2, HEADS_HERE):
        load_kv(i)
    for a, b in GREET:
        pl.when(z == a)(lambda: greet(device(b, y, core)))
    greet(sibling)
    for d in range(1, COLS):
        greet((seq, lax.rem(col + d, COLS)))

    for i, d in enumerate(order):
        pltpu.make_async_copy(q_hbm.at[:, columns_of(i)], q_s.at[row_peer(d)], misc_sem.at[2]).start()
    w_load.start()
    g_load.start()
    for level in range(3):

        @pl.when(jnp.logical_and(jnp.logical_not(z_bits[level]), z > 0))
        def _():
            high[:, mine, level * 128 : (level + 1) * 128] = jnp.zeros((HEADS_HERE, HALF, HEAD_DIM), BF16)

    @pl.when(jnp.logical_not(y_bits[2]))
    def _():
        high[:, :, 384:512] = jnp.zeros((HEADS_HERE, HEAD_DIM, HEAD_DIM), BF16)

    to_sibling = []
    for i, d in enumerate(order):
        h = row_peer(d)
        to_sibling.append(
            remote(own_sum.at[h, other, :], pair_in.at[h], pair_send, pair_recv.at[i], sibling)
        )
    for i, d in enumerate(order):
        h = row_peer(d)
        pltpu.make_async_copy(kv_s.at[h], kv_s.at[h], load_sem.at[i]).wait()
        k = kv_s[h, 0]
        v = kv_s[h, 1]
        s0 = tn(k[:STRETCH], v[:STRETCH])
        s1 = tn(k[STRETCH:], v[STRETCH:])
        first[h] = s0.astype(BF16)
        s = s0 + s1
        own_sum[h] = s
        own_bf[h] = s.astype(BF16)
        if i == 0:
            for row in range(RING):
                greeted = [a for a, b in GREET if b == row]

                @pl.when(z == row)
                def _():
                    pl.semaphore_wait(barrier, 1 + RING - 1 + COLS - 1 + len(greeted))
                    for a in [a for a, b in FORWARD if b == row]:
                        pl.semaphore_signal(
                            ready.at[TARGETS[a].index(row)], inc=1, device_id=device(a, y, core), device_id_type=MESH
                        )

        launch(to_sibling[i], alone=False)

    ends.append((None, remote(own_sum.at[:, other, :], pair_in, pair_send, pair_recv.at[0], sibling)))
    to_core1 = remote(own_bf, core0, core_send, core_recv, sibling)
    launch(to_core1, core == 0)

    def to_owner(d):
        h = row_peer(d)
        return remote(chip_sum.at[h], ring_in.at[y], ring_send, ring_recv, device(z, h, core))

    for i, d in enumerate(order):
        h = row_peer(d)
        to_sibling[i].wait_recv()
        c = (own_sum[h, mine, :] + pair_in[h]).astype(BF16)
        chip_sum[h] = c
        if d:
            launch(to_owner(d), alone=False)
        else:
            ring_in[y] = c

    def row_total(count, send, recv):
        return remote(chip_sum.at[0:count], ring_in.at[0:count], send, recv, device(z, row_peer(1), core))

    from_row = row_total(RING - 1, ring_send, ring_recv)
    ends.append((None, from_row))

    w_load.wait()
    for h in range(HEADS_HERE):
        for level in range(9):
            w_rows[h, level : level + 1, :] = w_v[level, h : h + 1, :]
        w_rows[h, 9:16, :] = jnp.zeros((7, TOK), F32)
    for h in range(HEADS_HERE):
        w_cols[h] = w_rows[h].T

    pltpu.make_async_copy(q_s, q_s, misc_sem.at[2]).wait()

    causal = lax.broadcasted_iota(jnp.int32, (STRETCH, STRETCH), 0) >= lax.broadcasted_iota(
        jnp.int32, (STRETCH, STRETCH), 1
    )

    def within(h):
        for s in range(2):
            rows = slice(s * STRETCH, (s + 1) * STRETCH)
            qs = q_s[h, rows, :]
            probs = jnp.where(causal, nt(qs, kv_s[h, 0, rows, :]), 0.0).astype(BF16)
            part = w_cols[h, rows, 0:1] * nn(probs, kv_s[h, 1, rows, :])
            if s == 1:
                part += w_cols[h, rows, 1:2] * nn(qs, first[h])
            acc[h, rows, :] = part

    for h in range(0, EARLY):
        within(h)

    to_next = remote(
        chip_sum, low.at[0, :, mine, :], next_send, next_recv, device(z, lax.rem(y + 1, RING), core)
    )
    launch(to_next, jnp.logical_not(y_bits[0]))

    from_row.wait_recv()
    part = [ring_in[j].astype(F32) for j in range(RING)]
    s01 = part[0] + part[1]
    s0123 = s01 + (part[2] + part[3])
    s45 = part[4] + part[5]
    totals[z] = s0123 + (s45 + (part[6] + part[7]))

    def to_row(a, b):
        sem = tot_send.at[TARGETS[a].index(b) if a < b else 3]
        first_in = min([c for c, t in PAIRS if t == b] or [0])
        return remote(totals.at[a], totals.at[a], sem, tot_recv.at[a - first_in], device(b, y, core))

    for a in TO_FIRST:
        launch(to_row(a, 0), z == a)
    for a, b in FORWARD:

        @pl.when(z == a)
        def _():
            pl.semaphore_wait(ready.at[TARGETS[a].index(b)], 1)

        if (a, b) in PAIRS:
            launch(to_row(a, b), z == a)

    ring_sum[0] = s01.astype(BF16)
    ring_sum[1] = s45.astype(BF16)
    ring_sum[2] = s0123.astype(BF16)

    def low_copy(level, d):
        target = row_peer(d)
        src = ring_sum.at[target // 4] if level == 1 else ring_sum.at[2]
        dst = low.at[1, y, mine, :] if level == 1 else high.at[y, mine, 384:512]
        return remote(
            src, dst, low_send.at[level - 1], low_recv.at[level - 1], device(z, target, core)
        )

    for d in FAR_FIRST:
        launch(low_copy(1, d), lax.rem(row_peer(d) // 2, 2) == 1, alone=False)
    for d in FAR_FIRST:
        launch(low_copy(2, d), jnp.logical_and(z == 0, row_peer(d) // 4 == 1), alone=False)
    for level in (1, 2):
        ends.append((y_bits[level], row_total(3, low_send.at[level - 1], ring_recv)))
        ends.append((jnp.logical_not(y_bits[level]), row_total(4, low_send.at[level - 1], ring_recv)))

    @pl.when(y_bits[1])
    def _():
        low[1, y, mine, :] = ring_sum[y // 4]

    @pl.when(y_bits[2])
    def _():
        high[y, mine, 384:512] = ring_sum[2]

    for h in range(EARLY, HEADS_HERE):
        within(h)

    level_lanes = [slice(level * 128, (level + 1) * 128) for level in range(3)]
    for row in range(RING):
        rows_in = [a for a, b in PAIRS if b == row] if row else list(TO_FIRST)
        level = len(rows_in).bit_length() - 1 if row else 2

        @pl.when(z == row)
        def _():
            for a in rows_in:
                to_row(a, row).wait_recv()
            state = totals[rows_in[0]]
            for a in rows_in[1:] + [0] * (row == 0):
                state = state + totals[a]
            high[y, mine, level_lanes[level]] = state.astype(BF16)

    lowest = (1 - lax.rem(z, 2)) * (2 - lax.rem(z // 2, 2))
    lanes = pl.ds(pl.multiple_of(lowest * 128, 128), 128)

    def along_row(d):
        return remote(
            high.at[y, mine, lanes], high.at[y, mine, lanes], high_send, high_recv.at[d - 1],
            device(z, row_peer(d), core),
        )

    for d in NEAR_FIRST:
        launch(along_row(d), alone=False)

    @pl.when(core == 1)
    def _():
        to_core1.wait_recv()
        for h in range(HEADS_HERE):
            acc[h] += w_cols[h, :, 2:3] * nn(q_s[h], core0[h])

    row_total(RING - 1, high_send, ring_recv).wait_send()
    for d in FAR_FIRST:
        launch(low_copy(2, d), jnp.logical_and(z > 0, row_peer(d) // 4 == 1), alone=False)

    def share_low(level):
        part = low.at[level, :, mine, :] if level < 2 else high.at[:, mine, 384:512]
        return remote(part, part, fwl_send.at[level], fwl_recv.at[level], sibling)

    def low_arrival(level, cond):
        @pl.when(cond)
        def _():
            if level == 0:
                to_next.wait_recv()
            else:
                row_total(RING - 1, ring_send, low_recv.at[level - 1]).wait_recv()
            share_low(level).start()

    for level in range(3):
        ends.append((y_bits[level], share_low(level)))
    low_arrival(0, y_bits[0])
    low_arrival(1, y_bits[1])
    low_arrival(2, jnp.logical_and(y_bits[2], z == 0))

    def low_readout(level):
        @pl.when(y_bits[level])
        def _():
            share_low(level).wait_recv()
            for h in range(HEADS_HERE):
                acc[h] += w_cols[h, :, 3 + level : 4 + level] * nn(q_s[h], low[level, h])

    arrivals = (0,) + NEAR_FIRST

    def share_high(i, h):
        part = high.at[h, mine, 0:384]
        return remote(part, part, fwh_send, fwh_recv.at[i], sibling)

    def hop(level, i, h, to):
        ref = high.at[h, mine, level_lanes[level]]
        return remote(ref, ref, up_send.at[level - 1], up_recv.at[level - 1, i], device(to, y, core))

    odd = z_bits[0]
    above = lax.rem(z + 1, RING)
    hop_in = {1: lax.rem(z, 4) == 3, 2: z > 4}
    @pl.when(z == 0)
    def _():
        low_readout(0)
        low_readout(1)
        pl.when(y_bits[2])(share_low(2).wait_recv)
        for h in range(HEADS_HERE):
            a = acc[h] + w_cols[h, :, 5:6] * nn(q_s[h], high[h, :, 384:512])
            acc[h] = a
            sq[...] = a * a if h == 0 else sq[...] + a * a

    for i, d in enumerate(arrivals):
        h = lax.rem(y + RING - d, RING)
        if d:
            pl.when(jnp.logical_not(odd))(along_row(d).wait_recv)
        for to in (RING - 2, RING - 1):
            launch(hop(2, i, h, to), z == 0, alone=False)
        launch(hop(2, i, h, above), z == 4, alone=False)
        launch(hop(1, i, h, above), lax.rem(z, 4) == 2, alone=False)
    ends.append((lax.rem(z, 4) == 2, row_total(RING, up_send.at[0], ring_recv)))
    ends.append((z == 4, row_total(RING, up_send.at[1], ring_recv)))
    ends.append((z == 0, remote(low.at[0], low.at[0], up_send.at[1], ring_recv, sibling)))

    def readout(i, d):
        h = lax.rem(y + RING - d, RING)
        share_high(i, h).wait_recv()
        r = nn(q_s[h], high[h])
        a = acc[h] + w_cols[h, :, 5:6] * r[:, 384:512]
        for level in range(3):
            a += w_cols[h, :, 6 + level : 7 + level] * r[:, level_lanes[level]]
        acc[h] = a
        sq[...] = a * a if i == 0 else sq[...] + a * a

    @pl.when(z > 0)
    def _():
        low_readout(0)
        low_readout(1)
        low_arrival(2, y_bits[2])
        for i, d in enumerate(arrivals):
            h = lax.rem(y + RING - d, RING)
            if d:
                pl.when(odd)(along_row(d).wait_recv)
            for level in (1, 2):
                pl.when(hop_in[level])(hop(level, i, h, above).wait_recv)
            share_high(i, h).start()
            if i == LAG:
                pl.when(y_bits[2])(share_low(2).wait_recv)
            if i >= LAG:
                readout(i - LAG, arrivals[i - LAG])
        for i in range(RING - LAG, RING):
            readout(i, arrivals[i])

    whole = high.at[:, mine, 0:384]
    ends.append((z > 0, remote(whole, whole, fwh_send, fwh_recv.at[0], sibling)))

    sq_in[col, 0:1, :] = jnp.sum(sq[...].T, axis=0, keepdims=True)

    def to_cols(d):
        return remote(
            sq_in.at[col, 0:1], sq_in.at[col, 0:1], sq_send, sq_recv,
            (seq, lax.rem(col + d, COLS)),
        )

    for d in (2, 1, 3):
        launch(to_cols(d), alone=False)
    g_load.wait()
    for h in range(HEADS_HERE):
        acc[h] = acc[h] * g_v[:, h * HEAD_DIM : (h + 1) * HEAD_DIM]
    others = sq_in.at[0 : COLS - 1, 0:1]
    from_cols = remote(others, others, sq_send, sq_recv, (seq, lax.rem(col + 1, COLS)))
    ends.append((None, from_cols))
    from_cols.wait_recv()
    squares = (sq_in[0, 0:1, :] + sq_in[1, 0:1, :]) + (sq_in[2, 0:1, :] + sq_in[3, 0:1, :])
    inverse = lax.rsqrt(squares / D + EPSILON)
    scale = jnp.broadcast_to(inverse, (HEAD_DIM, TOK)).T

    for h in range(HEADS_HERE):
        columns = slice(h * HEAD_DIM, (h + 1) * HEAD_DIM)
        out[:, columns] = (acc[h] * scale).astype(BF16)
    finish()


def local(queries, keys, values, level_weights, norm_gain):
    hd, tok, half, ring = HEAD_DIM, TOK, HALF, RING
    dma = pltpu.SemaphoreType.DMA
    any_space = pl.BlockSpec(memory_space=pl.ANY)
    scratch = [
        pltpu.VMEM((8, tok, hd), BF16),
        pltpu.VMEM((8, 2, tok, hd), BF16),
        pltpu.VMEM((9, 8, tok), F32),
        pltpu.VMEM((1, 1024), F32),
        pltpu.VMEM((8, 16, tok), F32),
        pltpu.VMEM((8, tok, 16), F32),
        pltpu.VMEM((8, hd, hd), BF16),
        pltpu.VMEM((8, hd, hd), F32),
        pltpu.VMEM((8, hd, hd), BF16),
        pltpu.VMEM((8, half, hd), F32),
        pltpu.VMEM((8, hd, hd), BF16),
        pltpu.VMEM((8, half, hd), BF16),
        pltpu.VMEM((ring, half, hd), BF16),
        pltpu.VMEM((3, half, hd), BF16),
        pltpu.VMEM((ring, half, hd), F32),
        pltpu.VMEM((2, 8, hd, hd), BF16),
        pltpu.VMEM((8, hd, 4 * hd), BF16),
        pltpu.VMEM((8, tok, hd), F32),
        pltpu.VMEM((tok, hd), F32),
        pltpu.VMEM((COLS, 8, tok), F32),
        dma((8,)), dma((3,)), pltpu.SemaphoreType.REGULAR((5,)),
        dma, dma((8,)), dma, dma, dma, dma, dma, dma,
        dma((2,)), dma((2,)), dma((4,)), dma((4,)), dma, dma((7,)), dma((2,)), dma((2, 8)),
        dma((3,)), dma((3,)), dma, dma((8,)), dma, dma,
    ]
    return pl.pallas_call(
        kernel,
        out_shape=pltpu.VMEM((tok, 8 * hd), BF16),
        in_specs=[any_space] * 5,
        out_specs=pl.BlockSpec(memory_space=pltpu.VMEM),
        scratch_shapes=scratch,
        compiler_params=pltpu.CompilerParams(
            collective_id=0, has_side_effects=True, vmem_limit_bytes=60 * 1024 * 1024
        ),
        cost_estimate=pl.CostEstimate(flops=2_000_000_000, bytes_accessed=4_400_000, transcendentals=0),
    )(queries, keys, values, level_weights, norm_gain.reshape(1, -1))


def solution(mesh):
    return jax.shard_map(
        local,
        mesh=mesh,
        in_specs=(
            P("seq", "head"),
            P("seq", "head"),
            P("seq", "head"),
            P(None, "head", "seq"),
            P("head"),
        ),
        out_specs=P("seq", "head"),
        check_vma=False,
    )
```
